256 devices in a mesh: hst: 64 (over y, z, core), grp: 4 (over x).
Axes of the slice: x: 4, y: 4, z: 8, core: 2. Of those that a mesh axis runs over, the one named last changes fastest.
Arguments:
- queries: bfloat16 [131072, 1536], P(('hst', 'grp')), may hold values from -5 to 5
- keys_values: bfloat16 [2, 131072, 1536], P(None, ('hst', 'grp')), may hold values from -5 to 5
- token_ids: int32 [131072], replicated, may hold values from 0 to 4095
- lengths: int32 [256], replicated, may hold values from 1 to 512, 98304 in all
- suffix_queries: bfloat16 [1024, 1536], P('hst', 'grp'), may hold values from -5 to 5
- suffix_kv: bfloat16 [2, 1024, 1536], P(None, 'hst', 'grp'), may hold values from -5 to 5
Outputs:
- context_out: bfloat16 [131072, 1536], P(('hst', 'grp'))
- suffix_out: bfloat16 [1024, 1536], P('hst', 'grp')
The draws below stay inside these ranges and needn't reach their ends.
All inputs are finite; a program needn't handle non-finite values.
Results may differ from the reference program's by a relative error of at most 0.0029.
Values may be sent and summed in bfloat16 or wider, within the bound.
A program may use at most 128 MiB of HBM per device.

```python
import math
import jax
import jax.numpy as jnp
import numpy as np
from jax import lax

HEADS = 12
HSZ = 128
VOC = 4096
BLK = 512
QS = 1024
HD = 1536
NAMB = 512
NBLK = 256
NTOK = 131072
N_HST = 64
N_GRP = 4


def query_law(key, rows):
    return jnp.clip(1.7 * jax.random.normal(key, (rows, HD)), -5.0, 5.0)


def key_law(key, rows):
    values = jnp.clip(jax.random.normal(jax.random.fold_in(key, 7), (rows, HD)), -5.0, 5.0)
    keys = jnp.clip(1.7 * jax.random.normal(key, (rows, HD)), -5.0, 5.0)
    return jnp.stack([keys, values]).astype(jnp.bfloat16)


def draw_queries(key, part):
    key = jax.random.fold_in(key, 1)
    return query_law(key, NTOK).astype(jnp.bfloat16)


def draw_keys_values(key, part):
    key = jax.random.fold_in(key, 2)
    return key_law(key, NTOK)


def draw_suffix_queries(key, part):
    key = jax.random.fold_in(key, 3)
    return query_law(key, QS).astype(jnp.bfloat16)


def draw_suffix_kv(key, part):
    key = jax.random.fold_in(key, 4)
    return key_law(key, QS)


def plant(array, rng, least, top_value):
    longest = array.shape.index(max(array.shape))
    spots = []
    for shift in (0, 1):
        where = [jax.random.randint(jax.random.fold_in(rng, axis), (), 0, length) for axis, length in enumerate(array.shape)]
        where[longest] = (where[longest] + shift) % array.shape[longest]
        spots.append(tuple(where))
    return array.at[spots[0]].set(least).at[spots[1]].set(top_value)


def profile(count, total, bound, lean):
    loads = [(1 << 20) // math.isqrt(grade ** lean) + 1 for grade in range(2, count + 1)]
    surplus, holding = total - bound - (count - 1), [1] * (count - 1)
    while surplus > 0:
        movable = [i for i in range(count - 1) if holding[i] < bound]
        whole, left = sum([loads[i] for i in movable]), surplus
        for i in movable:
            extra = min(bound - holding[i], max(1, left * loads[i] // whole), surplus)
            holding[i] = holding[i] + extra
            surplus = surplus - extra
    return np.array([bound] + holding)


def uneven_parts(own_key, number_of, total, reach, skew):
    if number_of == 2:
        one = jax.random.randint(own_key, (), max(1, total - reach), min(reach, total - 1) + 1)
        return jnp.stack([one, total - one])
    tallies = jnp.asarray(profile(number_of, total, reach, skew), jnp.int32)
    couples = (number_of - 1) // 2
    donor, sink = tallies[1:1 + 2 * couples:2], tallies[2:2 + 2 * couples:2]
    room = jnp.minimum(donor - 1, reach - sink)
    shifted = jax.random.randint(jax.random.fold_in(own_key, 1), (couples,), 0, 1 << 20) % (room + 1)
    tallies = tallies.at[1:1 + 2 * couples:2].set(donor - shifted).at[2:2 + 2 * couples:2].set(sink + shifted)
    return tallies[jax.random.permutation(jax.random.fold_in(own_key, 2), number_of)]


def setup_inputs(seed: int = 0) -> dict:
    streams_of = jax.random.split(jax.random.key(seed), 7)
    queries = draw_queries(jax.random.fold_in(streams_of[6], 71), 0)
    keys_values = draw_keys_values(jax.random.fold_in(streams_of[6], 71), 0)
    token_ids = plant(jax.random.randint(streams_of[2], (NTOK,), 0, VOC), jax.random.fold_in(streams_of[2], 1), 0, VOC - 1).astype(jnp.int32)
    lengths = uneven_parts(streams_of[3], NBLK, 3 * NBLK * BLK // 4, BLK, 2).astype(jnp.int32)
    suffix_queries = draw_suffix_queries(jax.random.fold_in(streams_of[6], 71), 0)
    suffix_kv = draw_suffix_kv(jax.random.fold_in(streams_of[6], 71), 0)
    return dict(queries=queries, keys_values=keys_values, token_ids=token_ids, lengths=lengths, suffix_queries=suffix_queries, suffix_kv=suffix_kv)


NEG = -1e+30

def attend(q, keys, values, valid):
    scale = 1.0 / math.sqrt(HSZ)
    s = jnp.einsum('qhd,khd->hqk', q, keys) * scale
    masked = jnp.where(valid[None], s, NEG)
    top = lax.optimization_barrier(jnp.max(masked, axis=-1))
    weights = jnp.where(valid[None], jnp.exp(masked - top[..., None]), 0.0)
    total = lax.optimization_barrier(jnp.sum(weights, axis=-1))
    rounded = lax.optimization_barrier(weights.astype(jnp.bfloat16))
    mixed = jnp.einsum('hqk,khd->qhd', rounded.astype(jnp.float32), values)
    return (top.T, total.T, mixed)

def reference(queries, keys_values, token_ids, lengths, suffix_queries, suffix_kv):
    clear = token_ids >= NAMB
    places = jnp.arange(BLK)
    anchor = keys_values[:, :BLK]
    anchor_ok = clear[:BLK] & (places < lengths[0])

    def context_block(block):
        start = block * BLK
        q = lax.dynamic_slice_in_dim(queries, start, BLK, 0).astype(jnp.float32).reshape(BLK, HEADS, HSZ)
        own = lax.dynamic_slice_in_dim(keys_values, start, BLK, 1)
        both = jnp.concatenate([anchor, own], axis=1).astype(jnp.float32).reshape(2, 2 * BLK, HEADS, HSZ)
        own_len = lengths[block]
        own_ok = lax.dynamic_slice_in_dim(clear, start, BLK, 0) & (places < own_len)
        causal = places[None, :] <= places[:, None]
        own_valid = causal & (own_ok[None, :] | (places[None, :] == places[:, None]))
        anchor_valid = jnp.broadcast_to((anchor_ok & (block > 0))[None, :], (BLK, BLK))
        valid = jnp.concatenate([anchor_valid, own_valid], axis=1)
        top, total, mixed = attend(q, both[0], both[1], valid)
        out = mixed / total[:, :, None]
        out = jnp.where((places < own_len)[:, None, None], out, 0.0)
        return out.astype(jnp.bfloat16).reshape(BLK, HD)
    context_out = lax.map(context_block, jnp.arange(N_HST * N_GRP)).reshape(NTOK, HD)
    span = N_GRP * BLK
    share = QS // N_HST
    width_q = min(512, QS)

    def group_step(carry, group):
        first = group * span
        ctx = lax.dynamic_slice_in_dim(keys_values, first, span, 1)
        suf = lax.dynamic_slice_in_dim(suffix_kv, group * share, share, 1)
        both = jnp.concatenate([ctx, suf], axis=1).astype(jnp.float32).reshape(2, span + share, HEADS, HSZ)
        lens = lax.dynamic_slice_in_dim(lengths, group * N_GRP, N_GRP, 0)
        ctx_ok = lax.dynamic_slice_in_dim(clear, first, span, 0) & (jnp.arange(span) % BLK < jnp.repeat(lens, BLK, total_repeat_length=span))
        spos = group * share + jnp.arange(share)

        def piece(index):
            q = lax.dynamic_slice_in_dim(suffix_queries, index * width_q, width_q, 0).astype(jnp.float32).reshape(width_q, HEADS, HSZ)
            qpos = index * width_q + jnp.arange(width_q)
            valid = jnp.concatenate([jnp.broadcast_to(ctx_ok[None, :], (width_q, span)), spos[None, :] <= qpos[:, None]], axis=1)
            return attend(q, both[0], both[1], valid)
        tops, totals, mixed = lax.map(piece, jnp.arange(QS // width_q))
        tops = tops.reshape(QS, HEADS)
        totals = totals.reshape(QS, HEADS)
        mixed = mixed.reshape(QS, HEADS, HSZ)
        best, summed, acc = carry
        upper = jnp.maximum(best, tops)
        old_factor = jnp.exp(best - upper)
        new_factor = jnp.exp(tops - upper)
        summed = summed * old_factor + totals * new_factor
        acc = acc * old_factor[..., None] + mixed * new_factor[..., None]
        return ((upper, summed, acc), None)
    start_state = (jnp.full((QS, HEADS), NEG, jnp.float32), jnp.zeros((QS, HEADS), jnp.float32), jnp.zeros((QS, HEADS, HSZ), jnp.float32))
    final, unused = lax.scan(group_step, start_state, jnp.arange(N_HST))
    suffix_out = (final[2] / final[1][..., None]).astype(jnp.bfloat16).reshape(QS, HD)
    return (context_out, suffix_out)
```

```python
import math

import jax
import jax.numpy as jnp
from jax import lax
from jax.experimental import pallas as pl
from jax.experimental.pallas import tpu as pltpu
from jax.sharding import PartitionSpec as P

HEADS = 12
HSZ = 128
BLK = 512
HD = HEADS * HSZ
NAMB = 512
NEG = -1e30
FLOOR = -1e29
SCALE2 = math.log2(math.e) / math.sqrt(HSZ)
CODE = 32767.0
SIZES = (4, 4, 8)
NX, NY, NZ = SIZES
GH = HEADS // NX
SHARE = 16
ROWS = NY * NZ * SHARE
YROWS = NZ * SHARE
TQ = 256
NT = (((1,), (1,)), ((), ()))
MESH = pl.DeviceIdType.MESH

DIRS = ((0, 1), (0, -1), (1, 1), (1, -1), (2, 1), (2, -1))
TREES = (
    ((1, 2, 0), (1, 1, 1)),
    ((1, 2, 0), (-1, 1, 1)),
    ((2, 0, 1), (-1, 1, 1)),
    ((2, 0, 1), (1, -1, 1)),
    ((2, 0, 1), (1, -1, -1)),
    ((0, 1, 2), (-1, 1, -1)),
)
MAXDEPTH = 9
NSLAB = 4


def rem(a, n):
    return lax.rem(a, jnp.int32(n))


def tree_root(k):
    axis, sign = DIRS[k]
    root = [0, 0, 0]
    root[axis] = sign % SIZES[axis]
    return root


def tree_plan(k, coords):
    order, signs = TREES[k]
    root = tree_root(k)
    u, depth = [], jnp.int32(1)
    for axis in range(3):
        n = SIZES[axis]
        r = rem(coords[axis] - root[axis] + n, n)
        if signs[axis] < 0:
            r = rem(n - r, n)
        u.append(r)
        depth = depth + jnp.where(r <= n // 2, r, n - r)
    sends = [None] * 6
    for place, axis in enumerate(order):
        n = SIZES[axis]
        there = jnp.bool_(True)
        for later in order[place + 1 :]:
            there = there & (u[later] == 0)
        far = there & (u[axis] < n // 2)
        near = there & ((u[axis] == 0) | (u[axis] > n // 2 + 1))
        plus, minus = (far, near) if signs[axis] > 0 else (near, far)
        sends[2 * axis] = plus
        sends[2 * axis + 1] = minus
    return depth, sends


def kernel(
    q_hbm, kv_hbm, tok_hbm, lens, sq_hbm, skv_hbm,
    ctx_hbm, suf_ref,
    q_v, kv_v, kvs, tok_v, sq_v, ksuf, qbuf, anc, acc1, m1, l1, own2d, bias, abias, sbias,
    codes, stats, ry, rys, codes2, stats2, rx, rxs, codes3, stats3, rz, rzs, obuf,
    in_sem, kvs_send, kvs_recv, sk_send, sk_recv,
    zq_send, zq_recv, yq_send, yq_recv, xq_send, xq_recv, xh_send, xh_recv,
    a_send, a_recv, s_send, s_recv, r_send,
    ry_send, ry_recv, rys_send, rys_recv, rx_send, rx_recv, rz_send, rz_recv,
    out_sem,
):
    hst = lax.axis_index("hst")
    x = lax.axis_index("grp")
    c = rem(hst, 2)
    z = rem(lax.div(hst, 2), NZ)
    y = lax.div(hst, 2 * NZ)
    block = hst * NX + x

    def dev(px, py, pz, pc):
        return ((py * NZ + pz) * 2 + pc, px)

    def xdev(delta):
        return dev(rem(x + delta, NX), y, z, c)

    def ydev(delta):
        return dev(x, rem(y + delta, NY), z, c)

    def zdev(delta):
        return dev(x, y, rem(z + delta, NZ), c)

    sibling = dev(x, y, z, 1 - c)
    neighbours = [xdev(1), xdev(NX - 1), ydev(1), ydev(NY - 1), zdev(1), zdev(NZ - 1)]

    def remote(src, dst, send, recv, to):
        return pltpu.make_async_remote_copy(
            src_ref=src, dst_ref=dst, send_sem=send, recv_sem=recv, device_id=to, device_id_type=MESH
        )

    sblock = (hst + 1 - 2 * c) * NX + x
    loads = [
        pltpu.make_async_copy(sq_hbm, sq_v, in_sem.at[0]),
        pltpu.make_async_copy(q_hbm, q_v, in_sem.at[1]),
        pltpu.make_async_copy(kv_hbm, kv_v, in_sem.at[2]),
        pltpu.make_async_copy(skv_hbm, ksuf.at[:, pl.ds(0, SHARE), :], in_sem.at[3]),
    ]
    for place, b in enumerate((block, sblock, 0)):
        first = pl.multiple_of(lax.div(b, 2) * 8, 8)
        loads.append(
            pltpu.make_async_copy(tok_hbm.at[pl.ds(first, 8), :], tok_v.at[place], in_sem.at[4 + place])
        )
    for copy in loads:
        copy.start()

    barrier = pltpu.get_barrier_semaphore()
    partners = [sibling]
    partners += [xdev(d) for d in range(1, NX)] + [ydev(d) for d in range(1, NY)]
    partners += [zdev(d) for d in range(1, NZ)]
    for partner in partners:
        pl.semaphore_signal(barrier, inc=1, device_id=partner, device_id_type=MESH)
    is_root = block == 0
    greeted = jnp.int32(len(partners))
    for k in range(3, 6):
        rx_, ry_, rz_ = tree_root(k)
        is_it = (x == rx_) & (y == ry_) & (z == rz_) & (c == 1)

        @pl.when(is_root)
        def _():
            pl.semaphore_signal(barrier, inc=1, device_id=dev(rx_, ry_, rz_, 1), device_id_type=MESH)

        @pl.when(is_it)
        def _():
            pl.semaphore_signal(barrier, inc=1, device_id=(0, 0), device_id_type=MESH)

        greeted = greeted + jnp.where(is_root | is_it, 1, 0)
    pl.semaphore_wait(barrier, greeted)

    loads[0].wait()
    qrow = pl.multiple_of((y * NZ + z) * SHARE, SHARE)
    for e in range(GH):
        qbuf[GH * x + e, pl.ds(qrow, SHARE), :] = sq_v[:, e * HSZ : (e + 1) * HSZ]
    zq = []
    for d in range(1, NZ):
        ref = qbuf.at[pl.ds(GH * x, GH), pl.ds(qrow, SHARE), :]
        zq.append(remote(ref, ref, zq_send.at[d - 1], zq_recv.at[d - 1], zdev(d)))
        zq[-1].start()

    kvs_copy = remote(kv_hbm, kvs, kvs_send, kvs_recv, sibling)
    kvs_copy.start()
    sk_copy = remote(skv_hbm, ksuf.at[:, pl.ds(SHARE, SHARE), :], sk_send, sk_recv, sibling)
    sk_copy.start()

    def slab_of(core, j, s):
        return rem(s, 2) * HEADS + 6 * core + 2 * j + lax.div(s, 2)

    def root_copy(k, s):
        core, j = k // 3, k % 3
        px, py, pz = tree_root(k)
        head = 6 * core + 2 * j + lax.div(s, 2)
        src = kv_hbm.at[rem(s, 2), :, pl.ds(pl.multiple_of(head * HSZ, HSZ), HSZ)]
        return remote(
            src, anc.at[slab_of(core, j, s)], r_send.at[k, s], a_recv.at[j, s], dev(px, py, pz, core)
        )

    @pl.when(is_root)
    def _():
        @pl.loop(0, NSLAB)
        def _(s):
            for k in range(6):
                root_copy(k, s).start()

    plans = []
    for j in range(3):
        depth0, sends0 = tree_plan(j, (x, y, z))
        depth1, sends1 = tree_plan(3 + j, (x, y, z))
        first = c == 0
        depth = jnp.where(first, depth0, depth1)
        sends = [(first & s0) | (~first & s1) for s0, s1 in zip(sends0, sends1)]
        plans.append((1 + lax.div(3 * (depth - 1), 2), sends))
    last_step = 1 + 3 * (MAXDEPTH - 1) // 2 + NSLAB

    def tree_copy(j, s, d):
        ref = anc.at[slab_of(c, j, s)]
        return remote(ref, ref, a_send.at[j, s, d], a_recv.at[j, s], neighbours[d])

    def sibling_copy(j, s, core):
        ref = anc.at[slab_of(core, j, s)]
        return remote(ref, ref, s_send.at[j, s], s_recv.at[j, s], sibling)

    def anchor_step(t):
        for j in range(3):
            place, sends = plans[j]
            s = t - place

            @pl.when((s >= 0) & (s < NSLAB))
            def _():
                tree_copy(j, s, 0).wait_recv()
                for d in range(6):

                    @pl.when(sends[d])
                    def _():
                        tree_copy(j, s, d).start()

                sibling_copy(j, s, c).start()

    for copy in loads[4:]:
        copy.wait()
    flat = lax.broadcasted_iota(jnp.int32, (4, HSZ), 0) * HSZ + lax.broadcasted_iota(jnp.int32, (4, HSZ), 1)

    def key_bias(place, b, length, on):
        both = tok_v[place]
        ids = jnp.where(rem(b, 2) == 1, both[4:8], both[0:4])
        part = jnp.where((ids >= NAMB) & (flat < length) & on, 0.0, NEG)
        return jnp.concatenate([part[i : i + 1] for i in range(4)], axis=1)

    own_len = lens[block]
    own_bias = key_bias(0, block, own_len, True)
    bias[:, 0:BLK] = own_bias
    bias[:, BLK:] = key_bias(1, sblock, lens[sblock], True)
    abias[...] = key_bias(2, jnp.int32(0), lens[0], block > 0)
    row2d = lax.broadcasted_iota(jnp.int32, (BLK, BLK), 0)
    col2d = lax.broadcasted_iota(jnp.int32, (BLK, BLK), 1)
    own2d[...] = jnp.where(col2d == row2d, 0.0, jnp.where(col2d < row2d, own_bias, NEG))
    krow = lax.broadcasted_iota(jnp.int32, (ROWS, HSZ), 0)
    klane = lax.broadcasted_iota(jnp.int32, (ROWS, HSZ), 1)
    qpos = lax.div(krow, SHARE) * (2 * SHARE) + c * SHARE + rem(krow, SHARE)
    kpos = jnp.where(klane < SHARE, hst * SHARE + klane, (hst + 1 - 2 * c) * SHARE + klane - SHARE)
    sbias[...] = jnp.where((klane < 2 * SHARE) & (kpos <= qpos), 0.0, NEG)
    ksuf[:, 2 * SHARE :, :] = jnp.zeros((2, HSZ - 2 * SHARE, GH * HSZ), ksuf.dtype)
    stats[...] = jnp.zeros_like(stats)

    def columns(h):
        return pl.ds(pl.multiple_of(h * HSZ, HSZ), HSZ)

    def wide(a, copies):
        return jnp.concatenate([a] * copies, axis=1)

    def pipelined(units, scores, finish):
        ready = scores(*units[0])
        for i, unit in enumerate(units):
            later = scores(*units[i + 1]) if i + 1 < len(units) else None
            finish(*unit, ready)
            ready = later

    def yq_block(py, first, rows):
        return qbuf.at[pl.ds(GH * x, GH), pl.ds(pl.multiple_of(py * YROWS + first, SHARE), rows), :]

    def yq_copy(py, first, rows, sem, delta):
        ref = yq_block(py, first, rows)
        return remote(ref, ref, yq_send.at[sem], yq_recv.at[sem], ydev(delta))

    yq_own = [yq_copy(y, 0, YROWS, 0, 1), yq_copy(y, 0, YROWS, 1, NY - 1)]
    below, above, over = rem(y + NY - 1, NY), rem(y + 1, NY), rem(y + 2, NY)
    yq_in = [yq_copy(below, 0, YROWS, 0, 1), yq_copy(above, 0, YROWS, 1, NY - 1)]
    half = YROWS // 2
    yq_on = [yq_copy(below, 0, half, 2, 1), yq_copy(above, half, half, 3, NY - 1)]
    yq_far = [yq_copy(over, 0, half, 2, 1), yq_copy(over, half, half, 3, NY - 1)]

    def xq_copy(px, e, way):
        ref = qbuf.at[GH * px + e]
        to = dev(rem(x + jnp.where(way == 0, 1, NX - 1), NX), y, z, c)
        return remote(ref, ref, xq_send.at[way, e], xq_recv.at[way, e], to)

    def xh_copy(px, e, way):
        ref = qbuf.at[GH * px + e, pl.ds(pl.multiple_of(way * (ROWS // 2), SHARE), ROWS // 2), :]
        to = dev(rem(x + jnp.where(way == 0, 1, NX - 1), NX), y, z, c)
        return remote(ref, ref, xh_send.at[way, e], xh_recv.at[way, e], to)

    loads[1].wait()
    loads[2].wait()

    def own_scores(h, t):
        q = q_v[t * TQ : (t + 1) * TQ, columns(h)]
        k = kv_v[0, 0 : (t + 1) * TQ, columns(h)]
        s = lax.dot_general(q, k, NT, preferred_element_type=jnp.float32)
        return s + own2d[t * TQ : (t + 1) * TQ, 0 : (t + 1) * TQ]

    def own_finish(h, t, s):
        rows = slice(t * TQ, (t + 1) * TQ)
        m = jnp.max(s, axis=1, keepdims=True)
        p = jnp.exp2((s - m) * SCALE2)
        v = kv_v[1, 0 : (t + 1) * TQ, columns(h)]
        l1[h, rows, :] = jnp.broadcast_to(jnp.sum(p, axis=1, keepdims=True), (TQ, HSZ))
        m1[h, rows, :] = jnp.broadcast_to(m, (TQ, HSZ))
        acc1[h, rows, :] = jnp.dot(p.astype(jnp.bfloat16), v, preferred_element_type=jnp.float32)

    @pl.loop(0, HEADS // 2)
    def _(t):
        @pl.when(t == 2)
        def _():
            for copy in zq:
                copy.wait_recv()
            for copy in yq_own:
                copy.start()

        @pl.when(t == 3)
        def _():
            for arrived, on in zip(yq_in, yq_on):
                arrived.wait_recv()
                on.start()

        @pl.when(t == 4)
        def _():
            for copy in yq_far:
                copy.wait_recv()
            for e in range(GH):
                for way in range(2):
                    xq_copy(x, e, way).start()

        anchor_step(t)
        pipelined([(2 * t + i, tile) for i in range(2) for tile in range(BLK // TQ)], own_scores, own_finish)

    sk_copy.wait_recv()
    loads[3].wait()
    kvs_copy.wait_recv()
    lane = lax.broadcasted_iota(jnp.int32, (TQ, HSZ), 1)

    def encode(o):
        a = jnp.maximum(jnp.max(jnp.abs(o), axis=-1, keepdims=True), 1e-30)
        return a, jnp.round(o * (CODE / a)).astype(jnp.int32).astype(jnp.int16)

    def suffix_head(h, e, own_group):
        def scores(t):
            q = qbuf[h, t * TQ : (t + 1) * TQ, :]
            parts = []
            for i, ref in enumerate((kv_v, kvs)):
                s = lax.dot_general(q, ref[0, :, columns(h)], NT, preferred_element_type=jnp.float32)
                parts.append(s + bias[:, i * BLK : (i + 1) * BLK])
            if own_group:
                s = lax.dot_general(q, ksuf[0, :, columns(e)], NT, preferred_element_type=jnp.float32)
                parts.append(s + sbias[t * TQ : (t + 1) * TQ, :])
            return jnp.concatenate(parts, axis=1)

        def finish(t, s):
            rows = slice(t * TQ, (t + 1) * TQ)
            m = jnp.maximum(jnp.max(s, axis=1, keepdims=True), FLOOR)
            p = jnp.exp2((s - m) * SCALE2)
            l = jnp.maximum(jnp.sum(p, axis=1, keepdims=True), 1.0)
            w = p.astype(jnp.bfloat16)
            o = jnp.dot(w[:, :BLK], kv_v[1, :, columns(h)], preferred_element_type=jnp.float32)
            o = o + jnp.dot(w[:, BLK : 2 * BLK], kvs[1, :, columns(h)], preferred_element_type=jnp.float32)
            if own_group:
                o = o + jnp.dot(w[:, 2 * BLK :], ksuf[1, :, columns(e)], preferred_element_type=jnp.float32)
            a, code = encode(o / l)
            codes[h, rows, :] = code
            lse = m * SCALE2 + jnp.log2(l)
            old = stats[rows, :]
            stats[rows, :] = jnp.where(lane == h, lse, jnp.where(lane == h + HSZ // 2, a, old))

        pipelined([(t,) for t in range(ROWS // TQ)], scores, finish)

    def ry_copy(h, d):
        to_row = pl.multiple_of(rem(y + d, NY) * YROWS, SHARE)
        return remote(
            codes.at[h, pl.ds(to_row, YROWS), :], ry.at[d - 1, h], ry_send.at[d - 1, h], ry_recv.at[d - 1, h], ydev(d)
        )

    @pl.loop(0, GH)
    def _(i):
        anchor_step(HEADS // 2 + i)
        h = GH * x + i
        suffix_head(h, i, True)
        for d in range(1, NY):
            ry_copy(h, d).start()

    @pl.loop(GH, HEADS)
    def _(i):
        anchor_step(HEADS // 2 + i)
        opposite = i >= 3 * GH
        way = rem(i - GH, 2)
        e = jnp.where(opposite, i - 3 * GH, lax.div(i - GH, 2))
        px = jnp.where(opposite, rem(x + 2, NX), rem(x + jnp.where(way == 0, NX - 1, 1), NX))

        @pl.when(jnp.logical_not(opposite))
        def _():
            xq_copy(px, e, way).wait_recv()
            xh_copy(px, e, way).start()

        @pl.when(opposite)
        def _():
            xh_copy(px, e, jnp.int32(0)).wait_recv()
            xh_copy(px, e, jnp.int32(1)).wait_recv()

        h = GH * px + e
        suffix_head(h, e, False)
        for d in range(1, NY):
            ry_copy(h, d).start()

    def rys_copy(d):
        to_row = pl.multiple_of(rem(y + d, NY) * YROWS, SHARE)
        return remote(stats.at[pl.ds(to_row, YROWS), :], rys.at[d - 1], rys_send.at[d - 1], rys_recv.at[d - 1], ydev(d))

    for d in range(1, NY):
        rys_copy(d).start()

    def merge(parts):
        top = parts[0]
        for s in parts[1:]:
            top = jnp.maximum(top, s)
        weights = [jnp.exp2(s - top) for s in parts]
        total = weights[0]
        for w in weights[1:]:
            total = total + w
        inverse = 1.0 / (total * CODE)
        coefficients = [w * inverse * pltpu.roll(s, HSZ // 2, 1) for w, s in zip(weights, parts)]
        return top + jnp.log2(total), coefficients

    def pick(a, h):
        there = lax.broadcasted_iota(jnp.int32, a.shape, 1) == h
        return jnp.sum(jnp.where(there, a, 0.0), axis=1, keepdims=True)

    def blend(coefficients, coded, h):
        total = None
        for coefficient, code in zip(coefficients, coded):
            term = pick(coefficient, h) * code.astype(jnp.int32).astype(jnp.float32)
            total = term if total is None else total + term
        return total

    def reduce_y():
        for d in range(1, NY):
            rys_copy(d).wait_recv()

        @pl.loop(0, HEADS)
        def _(h):
            for d in range(1, NY):
                ry_copy(h, d).wait_recv()

        own_rows = pl.ds(pl.multiple_of(y * YROWS, SHARE), YROWS)
        lse, coefficients = merge([stats[own_rows, :]] + [rys[d] for d in range(NY - 1)])
        stats2[...] = lse
        lanes = lax.broadcasted_iota(jnp.int32, (YROWS, HSZ), 1)

        @pl.loop(0, HEADS)
        def _(h):
            o = blend(coefficients, [codes[h, own_rows, :]] + [ry[d, h] for d in range(NY - 1)], h)
            a, code = encode(o)
            codes2[h] = code
            stats2[...] = jnp.where(lanes == h + HSZ // 2, a, stats2[...])

    def rx_copies(d):
        px = rem(x + d, NX)
        return [
            remote(codes2.at[pl.ds(GH * px, GH)], rx.at[d - 1], rx_send.at[0, d - 1], rx_recv.at[0, d - 1], xdev(d)),
            remote(stats2, rxs.at[d - 1], rx_send.at[1, d - 1], rx_recv.at[1, d - 1], xdev(d)),
        ]

    def reduce_x():
        for d in range(1, NX):
            for copy in rx_copies(d):
                copy.wait_recv()
        lse, coefficients = merge([stats2[...]] + [rxs[d] for d in range(NX - 1)])
        lanes = lax.broadcasted_iota(jnp.int32, (YROWS, HSZ), 1)
        for e in range(GH):
            h = GH * x + e
            o = blend(coefficients, [codes2[h]] + [rx[d, e] for d in range(NX - 1)], h)
            a, code = encode(o)
            codes3[e] = code
            lse = jnp.where(lanes == h + HSZ // 2, a, lse)
        stats3[...] = lse

    def rz_copies(d):
        rows = pl.ds(pl.multiple_of(rem(z + d, NZ) * SHARE, SHARE), SHARE)
        return [
            remote(codes3.at[:, rows, :], rz.at[d - 1], rz_send.at[0, d - 1], rz_recv.at[0, d - 1], zdev(d)),
            remote(stats3.at[rows, :], rzs.at[d - 1], rz_send.at[1, d - 1], rz_recv.at[1, d - 1], zdev(d)),
        ]

    def reduce_z():
        for d in range(1, NZ):
            for copy in rz_copies(d):
                copy.wait_recv()
        rows = pl.ds(pl.multiple_of(z * SHARE, SHARE), SHARE)
        unused, coefficients = merge([stats3[rows, :]] + [rzs[d] for d in range(NZ - 1)])
        for e in range(GH):
            o = blend(coefficients, [codes3[e, rows, :]] + [rz[d, e] for d in range(NZ - 1)], GH * x + e)
            suf_ref[:, e * HSZ : (e + 1) * HSZ] = o.astype(suf_ref.dtype)

    @pl.loop(HEADS // 2 + HEADS, last_step)
    def _(t):
        anchor_step(t)

    @pl.loop(0, NSLAB)
    def _(s):
        for j in range(3):
            sibling_copy(j, s, 1 - c).wait_recv()

    def anchor_scores(h, t):
        q = q_v[t * TQ : (t + 1) * TQ, columns(h)]
        return lax.dot_general(q, anc[h], NT, preferred_element_type=jnp.float32) + abias[...]

    def anchor_finish(h, t, s):
        rows = slice(t * TQ, (t + 1) * TQ)
        before = m1[h, rows, :]
        m = jnp.maximum(before, jnp.max(s, axis=1, keepdims=True))
        p = jnp.exp2((s - wide(m, BLK // HSZ)) * SCALE2)
        fade = jnp.exp2((before - m) * SCALE2)
        l = l1[h, rows, :] * fade + jnp.sum(p, axis=1, keepdims=True)
        o = jnp.dot(p.astype(jnp.bfloat16), anc[HEADS + h], preferred_element_type=jnp.float32)
        o = (acc1[h, rows, :] * fade + o) / l
        place = lax.broadcasted_iota(jnp.int32, (TQ, HSZ), 0) + t * TQ
        obuf[h, rows, :] = jnp.where(place < own_len, o, 0.0).astype(obuf.dtype)

    def out_copy(h):
        return pltpu.make_async_copy(obuf.at[h], ctx_hbm.at[:, columns(h)], out_sem.at[h])

    @pl.loop(0, HEADS // 2)
    def _(t):
        @pl.when(t == 2)
        def _():
            reduce_y()
            for d in range(1, NX):
                for copy in rx_copies(d):
                    copy.start()

        @pl.when(t == 4)
        def _():
            reduce_x()
            for d in range(1, NZ):
                for copy in rz_copies(d):
                    copy.start()

        pipelined([(2 * t + i, tile) for i in range(2) for tile in range(BLK // TQ)], anchor_scores, anchor_finish)
        for i in range(2):
            out_copy(2 * t + i).start()

    reduce_z()

    for copy in zq + yq_own + yq_on + [kvs_copy, sk_copy]:
        copy.wait_send()

    @pl.loop(0, GH)
    def _(e):
        for way in range(2):
            xq_copy(x, e, jnp.int32(way)).wait_send()
            xh_copy(x, e, jnp.int32(way)).wait_send()

    @pl.loop(0, NSLAB)
    def _(s):
        for j in range(3):
            for d in range(6):

                @pl.when(plans[j][1][d])
                def _():
                    tree_copy(j, s, d).wait_send()

            sibling_copy(j, s, c).wait_send()

    @pl.when(is_root)
    def _():
        @pl.loop(0, NSLAB)
        def _(s):
            for k in range(6):
                root_copy(k, s).wait_send()

    @pl.loop(0, HEADS)
    def _(h):
        for d in range(1, NY):
            ry_copy(h, d).wait_send()
        out_copy(h).wait()

    for d in range(1, NY):
        rys_copy(d).wait_send()
    for d in range(1, NX):
        for copy in rx_copies(d):
            copy.wait_send()
    for d in range(1, NZ):
        for copy in rz_copies(d):
            copy.wait_send()


def per_device(queries, keys_values, token_ids, lengths, suffix_queries, suffix_kv):
    bf16, f32, i16 = jnp.bfloat16, jnp.float32, jnp.int16
    dma = pltpu.SemaphoreType.DMA
    scratch = [
        pltpu.VMEM((BLK, HD), bf16),
        pltpu.VMEM((2, BLK, HD), bf16),
        pltpu.VMEM((2, BLK, HD), bf16),
        pltpu.VMEM((3, 8, HSZ), jnp.int32),
        pltpu.VMEM((SHARE, GH * HSZ), bf16),
        pltpu.VMEM((2, HSZ, GH * HSZ), bf16),
        pltpu.VMEM((HEADS, ROWS, HSZ), bf16),
        pltpu.VMEM((2 * HEADS, BLK, HSZ), bf16),
        pltpu.VMEM((HEADS, BLK, HSZ), f32),
        pltpu.VMEM((HEADS, BLK, HSZ), f32),
        pltpu.VMEM((HEADS, BLK, HSZ), f32),
        pltpu.VMEM((BLK, BLK), f32),
        pltpu.VMEM((1, 2 * BLK), f32),
        pltpu.VMEM((1, BLK), f32),
        pltpu.VMEM((ROWS, HSZ), f32),
        pltpu.VMEM((HEADS, ROWS, HSZ), i16),
        pltpu.VMEM((ROWS, HSZ), f32),
        pltpu.VMEM((NY - 1, HEADS, YROWS, HSZ), i16),
        pltpu.VMEM((NY - 1, YROWS, HSZ), f32),
        pltpu.VMEM((HEADS, YROWS, HSZ), i16),
        pltpu.VMEM((YROWS, HSZ), f32),
        pltpu.VMEM((NX - 1, GH, YROWS, HSZ), i16),
        pltpu.VMEM((NX - 1, YROWS, HSZ), f32),
        pltpu.VMEM((GH, YROWS, HSZ), i16),
        pltpu.VMEM((YROWS, HSZ), f32),
        pltpu.VMEM((NZ - 1, GH, SHARE, HSZ), i16),
        pltpu.VMEM((NZ - 1, SHARE, HSZ), f32),
        pltpu.VMEM((HEADS, BLK, HSZ), bf16),
        dma((7,)),
        dma, dma, dma, dma,
        dma((NZ - 1,)), dma((NZ - 1,)),
        dma((4,)), dma((4,)),
        dma((2, GH)), dma((2, GH)),
        dma((2, GH)), dma((2, GH)),
        dma((3, NSLAB, 6)), dma((3, NSLAB)),
        dma((3, NSLAB)), dma((3, NSLAB)),
        dma((6, NSLAB)),
        dma((NY - 1, HEADS)), dma((NY - 1, HEADS)),
        dma((NY - 1,)), dma((NY - 1,)),
        dma((2, NX - 1)), dma((2, NX - 1)),
        dma((2, NZ - 1)), dma((2, NZ - 1)),
        dma((HEADS,)),
    ]
    anywhere = pl.BlockSpec(memory_space=pl.ANY)
    return pl.pallas_call(
        kernel,
        out_shape=(
            jax.ShapeDtypeStruct((BLK, HD), bf16),
            jax.ShapeDtypeStruct((SHARE, GH * HSZ), bf16),
        ),
        in_specs=[anywhere, anywhere, anywhere, pl.BlockSpec(memory_space=pltpu.SMEM), anywhere, anywhere],
        out_specs=(anywhere, pl.BlockSpec(memory_space=pltpu.VMEM)),
        scratch_shapes=scratch,
        compiler_params=pltpu.CompilerParams(
            collective_id=0, has_side_effects=True, vmem_limit_bytes=56 * 2**20
        ),
        cost_estimate=pl.CostEstimate(
            flops=6_500_000_000, bytes_accessed=6_500_000, transcendentals=12_600_000
        ),
        name="star",
    )(queries, keys_values, token_ids.reshape(-1, HSZ), lengths, suffix_queries, suffix_kv)


def solution(mesh):
    return jax.shard_map(
        per_device,
        mesh=mesh,
        in_specs=(
            P(("hst", "grp"), None),
            P(None, ("hst", "grp"), None),
            P(),
            P(),
            P("hst", "grp"),
            P(None, "hst", "grp"),
        ),
        out_specs=(P(("hst", "grp"), None), P("hst", "grp")),
        check_vma=False,
    )
```

```python
import math

import jax
import jax.numpy as jnp
from jax import lax
from jax.experimental import pallas as pl
from jax.experimental.pallas import tpu as pltpu
from jax.sharding import PartitionSpec as P

HEADS = 12
HSZ = 128
BLK = 512
HD = HEADS * HSZ
NAMB = 512
NEG = -1e30
FLOOR = -1e29
SCALE2 = math.log2(math.e) / math.sqrt(HSZ)
CODE = 32767.0
SIZES = (4, 4, 8)
NX, NY, NZ = SIZES
GH = HEADS // NX
SHARE = 16
QB = NZ * SHARE
TQ = 256
NCH = 3
CW = HD // 2 // NCH
PROWS = BLK // (NX * NY)
AROWS = BLK // NX
NT = (((1,), (1,)), ((), ()))
MESH = pl.DeviceIdType.MESH


def rem(a, n):
    return lax.rem(a, jnp.int32(n))


def kernel(
    q_hbm, kv_hbm, tok_hbm, lens, sq_hbm, skv_hbm,
    ctx_hbm, suf_ref,
    q_v, kv_v, kvs, tok_v, ksuf, qbuf, anc, stage, acc1, m1, l1, own2d, bias, abias,
    codes, stats, rb, rbs, codes2, stats2, ra, ras, codes3, stats3, rz, rzs, turned, obuf,
    in_sem, kvs_send, kvs_recv, sk_send, sk_recv,
    zq_send, zq_recv, bq_send, bq_recv, aq_send, aq_recv,
    sc_send, sc_recv, own_sem, sb_send, sb_recv, zb_send, zb_recv, bb_send, bb_recv, ab_send, ab_recv, sib_send, sib_recv,
    rb_send, rb_recv, ra_send, ra_recv, rz_send, rz_recv,
    out_sem,
):
    hst = lax.axis_index("hst")
    x = lax.axis_index("grp")
    c = rem(hst, 2)
    z = rem(lax.div(hst, 2), NZ)
    y = lax.div(hst, 2 * NZ)
    block = hst * NX + x
    first = c == 0
    ca = jnp.where(first, x, y)
    cb = jnp.where(first, y, x)

    def dev(px, py, pz, pc):
        return ((py * NZ + pz) * 2 + pc, px)

    def place(pa, pb, pz, pc):
        on = pc == 0
        return dev(jnp.where(on, pa, pb), jnp.where(on, pb, pa), pz, pc)

    def adev(delta):
        return place(rem(ca + delta, NX), cb, z, c)

    def bdev(delta):
        return place(ca, rem(cb + delta, NX), z, c)

    def zdev(delta):
        return dev(x, y, rem(z + delta, NZ), c)

    sibling = dev(x, y, z, 1 - c)

    def remote(src, dst, send, recv, to):
        return pltpu.make_async_remote_copy(
            src_ref=src, dst_ref=dst, send_sem=send, recv_sem=recv, device_id=to, device_id_type=MESH
        )

    sblock = (hst + 1 - 2 * c) * NX + x
    zrow = pl.multiple_of(z * SHARE, SHARE)
    qloads = [
        pltpu.make_async_copy(
            sq_hbm.at[:, pl.ds(e * HSZ, HSZ)], qbuf.at[ca, cb, e, pl.ds(zrow, SHARE), :], in_sem.at[6 + e]
        )
        for e in range(GH)
    ]
    loads = [
        pltpu.make_async_copy(q_hbm, q_v, in_sem.at[0]),
        pltpu.make_async_copy(kv_hbm, kv_v, in_sem.at[1]),
        pltpu.make_async_copy(skv_hbm, ksuf.at[:, pl.ds(0, SHARE), :], in_sem.at[2]),
    ]
    for i, b in enumerate((block, sblock, 0)):
        row = pl.multiple_of(lax.div(b, 2) * 8, 8)
        loads.append(pltpu.make_async_copy(tok_hbm.at[pl.ds(row, 8), :], tok_v.at[i], in_sem.at[3 + i]))
    for copy in qloads + loads:
        copy.start()

    barrier = pltpu.get_barrier_semaphore()
    partners = [sibling]
    partners += [adev(d) for d in range(1, NX)] + [bdev(d) for d in range(1, NY)]
    partners += [zdev(d) for d in range(1, NZ)]
    for partner in partners:
        pl.semaphore_signal(barrier, inc=1, device_id=partner, device_id_type=MESH)
    is_root = block == 0
    is_extra = (z == 0) & (x == 0) & (y > 0) & (c == 1)

    @pl.when(is_extra)
    def _():
        pl.semaphore_signal(barrier, inc=1, device_id=(0, 0), device_id_type=MESH)

    pl.semaphore_wait(barrier, len(partners) + jnp.where(is_root, NY - 1, 0))

    for copy in qloads:
        copy.wait()
    zq = []
    for d in range(1, NZ):
        ref = qbuf.at[ca, cb, :, pl.ds(zrow, SHARE), :]
        zq.append(remote(ref, ref, zq_send.at[d - 1], zq_recv.at[d - 1], zdev(d)))
        zq[-1].start()

    kvs_copy = remote(kv_hbm, kvs, kvs_send, kvs_recv, sibling)
    kvs_copy.start()
    sk_copy = remote(skv_hbm, ksuf.at[:, pl.ds(SHARE, SHARE), :], sk_send, sk_recv, sibling)
    sk_copy.start()

    def piece(ref, k, pa, pb, core, rows):
        row = pl.multiple_of(pa * AROWS + pb * PROWS, PROWS)
        col = pl.multiple_of(core * (HD // 2) + k * CW, HSZ)
        return ref.at[:, pl.ds(row, rows), pl.ds(col, CW)]

    def scatter_copy(k, i):
        core, pa = rem(i, 2), lax.div(i, 2)
        src = piece(kv_hbm, k, pa, 0, core, AROWS)
        return remote(src, stage.at[k], sc_send.at[k, i], sc_recv.at[k], place(pa, 0, 0, core))

    def root_own(k):
        return pltpu.make_async_copy(piece(kv_hbm, k, 0, 0, 0, AROWS), stage.at[k], own_sem.at[k])

    @pl.when(is_root)
    def _():
        for k in range(NCH):
            root_own(k).start()
            for i in (4, 5, 2, 3, 6, 7, 1):
                scatter_copy(k, jnp.int32(i)).start()

    def sb_copy(k, d):
        src = stage.at[k, :, pl.ds(d * PROWS, PROWS), :]
        return remote(src, piece(anc, k, ca, rem(cb + d, NX), c, PROWS), sb_send.at[k, d - 1], sb_recv.at[k], bdev(d))

    def zb_copy(k, d):
        ref = piece(anc, k, ca, cb, c, PROWS)
        return remote(ref, ref, zb_send.at[k, d - 1], zb_recv.at[k], zdev(d))

    def bb_copy(k, pb, d):
        ref = piece(anc, k, ca, pb, c, PROWS)
        return remote(ref, ref, bb_send.at[k, d - 1], bb_recv.at[k, d - 1], bdev(d))

    def ab_copy(k, pa, d):
        ref = piece(anc, k, pa, 0, c, AROWS)
        return remote(ref, ref, ab_send.at[k, d - 1], ab_recv.at[k, d - 1], adev(d))

    def sib_copy(k, core):
        ref = piece(anc, k, 0, 0, core, BLK)
        return remote(ref, ref, sib_send.at[k], sib_recv.at[k], sibling)

    def anchor_first(k):
        @pl.when((z == 0) & (cb == 0))
        def _():
            @pl.when(is_root)
            def _():
                root_own(k).wait()

            @pl.when(jnp.logical_not(is_root))
            def _():
                remote(stage.at[k], stage.at[k], sib_send.at[k], sc_recv.at[k], sibling).wait_recv()

            for d in (2, 1, 3):
                sb_copy(k, d).start()
            row = pl.multiple_of(ca * AROWS, AROWS)
            col = pl.multiple_of(c * (HD // 2) + k * CW, HSZ)
            anc[:, pl.ds(row, PROWS), pl.ds(col, CW)] = stage[k, :, 0:PROWS, :]

    def anchor_second(k):
        @pl.when(z == 0)
        def _():
            @pl.when(cb > 0)
            def _():
                ref = piece(anc, k, ca, cb, c, PROWS)
                remote(ref, ref, sib_send.at[k], sb_recv.at[k], sibling).wait_recv()

            for d in (4, 3, 5, 2, 6, 1, 7):
                zb_copy(k, d).start()

    def anchor_z(k):
        @pl.when(z > 0)
        def _():
            zb_copy(k, 1).wait_recv()

        for d in (2, 1, 3):
            bb_copy(k, cb, d).start()

    def anchor_b(k):
        for d in range(1, NX):
            bb_copy(k, rem(cb + NX - d, NX), d).wait_recv()
        for d in (2, 1, 3):
            ab_copy(k, ca, d).start()

    def anchor_a(k):
        for d in range(1, NX):
            ab_copy(k, rem(ca + NX - d, NX), d).wait_recv()
        sib_copy(k, c).start()

    for copy in loads[3:]:
        copy.wait()
    flat = lax.broadcasted_iota(jnp.int32, (4, HSZ), 0) * HSZ + lax.broadcasted_iota(jnp.int32, (4, HSZ), 1)

    def key_bias(i, b, length, on):
        both = tok_v[i]
        ids = jnp.where(rem(b, 2) == 1, both[4:8], both[0:4])
        part = jnp.where((ids >= NAMB) & (flat < length) & on, 0.0, NEG)
        return jnp.concatenate([part[r : r + 1] for r in range(4)], axis=1)

    own_len = lens[block]
    own_bias = key_bias(0, block, own_len, True)
    bias[:, 0:BLK] = own_bias
    bias[:, BLK:] = key_bias(1, sblock, lens[sblock], True)
    abias[...] = key_bias(2, jnp.int32(0), lens[0], block > 0)
    row2d = lax.broadcasted_iota(jnp.int32, (BLK, BLK), 0)
    col2d = lax.broadcasted_iota(jnp.int32, (BLK, BLK), 1)
    own2d[...] = jnp.where(col2d == row2d, 0.0, jnp.where(col2d < row2d, own_bias, NEG))
    ksuf[:, 2 * SHARE :, :] = jnp.zeros((2, HSZ - 2 * SHARE, GH * HSZ), ksuf.dtype)

    def columns(h):
        return pl.ds(pl.multiple_of(h * HSZ, HSZ), HSZ)

    def wide(a, copies):
        return jnp.concatenate([a] * copies, axis=1)

    def pipelined(units, scores, finish):
        ready = scores(*units[0])
        for i, unit in enumerate(units):
            later = scores(*units[i + 1]) if i + 1 < len(units) else None
            finish(*unit, ready)
            ready = later

    loads[0].wait()
    loads[1].wait()

    def own_scores(h, t):
        q = q_v[t * TQ : (t + 1) * TQ, columns(h)]
        k = kv_v[0, 0 : (t + 1) * TQ, columns(h)]
        s = lax.dot_general(q, k, NT, preferred_element_type=jnp.float32)
        return s + own2d[t * TQ : (t + 1) * TQ, 0 : (t + 1) * TQ]

    def own_finish(h, t, s):
        rows = slice(t * TQ, (t + 1) * TQ)
        m = jnp.max(s, axis=1, keepdims=True)
        p = jnp.exp2((s - m) * SCALE2)
        v = kv_v[1, 0 : (t + 1) * TQ, columns(h)]
        l1[h, rows, :] = jnp.broadcast_to(jnp.sum(p, axis=1, keepdims=True), (TQ, HSZ))
        m1[h, rows, :] = jnp.broadcast_to(m, (TQ, HSZ))
        acc1[h, rows, :] = jnp.dot(p.astype(jnp.bfloat16), v, preferred_element_type=jnp.float32)

    @pl.loop(0, HEADS // 2)
    def _(t):
        pipelined([(2 * t + i, tile) for i in range(2) for tile in range(BLK // TQ)], own_scores, own_finish)

    def bq_copy(pb, d):
        ref = qbuf.at[ca, pb]
        return remote(ref, ref, bq_send.at[d - 1], bq_recv.at[d - 1], bdev(d))

    def aq_copy(pa, pb, d):
        ref = qbuf.at[pa, pb]
        return remote(ref, ref, aq_send.at[d - 1, pb], aq_recv.at[d - 1, pb], adev(d))

    for copy in zq:
        copy.wait_recv()
    for d in (2, 1, 3):
        bq_copy(cb, d).start()
    for d in (2, 1, 3):
        aq_copy(ca, cb, d).start()
    anchor_first(0)
    anchor_first(1)

    sk_copy.wait_recv()
    loads[2].wait()
    lane = lax.broadcasted_iota(jnp.int32, (QB, HSZ), 1)
    pair_lane = lax.broadcasted_iota(jnp.int32, (2 * QB, HSZ), 1)
    pair_row = lax.broadcasted_iota(jnp.int32, (2 * QB, HSZ), 0)

    def encode(o):
        a = jnp.maximum(jnp.max(jnp.abs(o), axis=-1, keepdims=True), 1e-30)
        return a, jnp.round(o * (CODE / a)).astype(jnp.int32).astype(jnp.int16)

    def suffix_pair(blocks, with_suffix):
        bx = jnp.where(first, *blocks[0])
        bys = [jnp.where(first, ib, ia) for ia, ib in blocks]

        def scores(e):
            q = jnp.concatenate([qbuf[ia, ib, e] for ia, ib in blocks], axis=0)
            parts = []
            for i, ref in enumerate((kv_v, kvs)):
                s = lax.dot_general(q, ref[0, :, columns(GH * bx + e)], NT, preferred_element_type=jnp.float32)
                parts.append(s + bias[:, i * BLK : (i + 1) * BLK])
            if with_suffix:
                by = jnp.where(pair_row < QB, bys[0], bys[1] - 1)
                qpos = by * (2 * QB) + lax.div(pair_row, SHARE) * (2 * SHARE) + c * SHARE + rem(pair_row, SHARE)
                other = (hst + 1 - 2 * c) * SHARE + pair_lane - SHARE
                kpos = jnp.where(pair_lane < SHARE, hst * SHARE + pair_lane, other)
                s = lax.dot_general(q, ksuf[0, :, e * HSZ : (e + 1) * HSZ], NT, preferred_element_type=jnp.float32)
                parts.append(jnp.where((pair_lane < 2 * SHARE) & (kpos <= qpos), s, NEG))
            return jnp.concatenate(parts, axis=1)

        columns_of = []

        def finish(e, s):
            m = jnp.maximum(jnp.max(s, axis=1, keepdims=True), FLOOR)
            p = jnp.exp2((s - m) * SCALE2)
            l = jnp.maximum(jnp.sum(p, axis=1, keepdims=True), 1.0)
            w = p.astype(jnp.bfloat16)
            h = GH * bx + e
            o = jnp.dot(w[:, :BLK], kv_v[1, :, columns(h)], preferred_element_type=jnp.float32)
            o = o + jnp.dot(w[:, BLK : 2 * BLK], kvs[1, :, columns(h)], preferred_element_type=jnp.float32)
            if with_suffix:
                v = ksuf[1, :, e * HSZ : (e + 1) * HSZ]
                o = o + jnp.dot(w[:, 2 * BLK :], v, preferred_element_type=jnp.float32)
            a, code = encode(o / l)
            lse = m * SCALE2 + jnp.log2(l)
            for i, (ia, ib) in enumerate(blocks):
                codes[ia, ib, e] = code[i * QB : (i + 1) * QB]
            columns_of.append((lse, a))

        pipelined([(e,) for e in range(GH)], scores, finish)
        for i, (ia, ib) in enumerate(blocks):
            rows = slice(i * QB, (i + 1) * QB)
            stats[ia, ib] = rows_of([(lse[rows], a[rows]) for lse, a in columns_of])

    def rows_of(columns_of):
        flat_stats = jnp.zeros((QB, HSZ), jnp.float32)
        for e, (lse, a) in enumerate(columns_of):
            flat_stats = jnp.where(lane == e, lse, jnp.where(lane == 4 + e, a, flat_stats))
        return flat_stats.T[0:8]

    def merge(parts):
        lses = [s[0:4] for s in parts]
        top = lses[0]
        for s in lses[1:]:
            top = jnp.maximum(top, s)
        weights = [jnp.exp2(s - top) for s in lses]
        total = weights[0]
        for w in weights[1:]:
            total = total + w
        inverse = 1.0 / (total * CODE)
        rows = jnp.concatenate([w * inverse * s[4:8] for w, s in zip(weights, parts)], axis=0)
        rows = jnp.concatenate([rows, jnp.zeros((HSZ - rows.shape[0], HSZ), jnp.float32)], axis=0)
        return rows.T, top + jnp.log2(total)

    def blend(coefficients, coded, e):
        total = None
        for i, code in enumerate(coded):
            term = coefficients[:, 4 * i + e : 4 * i + e + 1] * code.astype(jnp.int32).astype(jnp.float32)
            total = term if total is None else total + term
        return total

    def blend_and_encode(parts, coded_of, store):
        coefficients, lse = merge(parts)
        scales = []
        for e in range(GH):
            a, code = encode(blend(coefficients, coded_of(e), e))
            store(e, code)
            scales.append((a, a))
        return jnp.concatenate([lse, rows_of(scales)[0:4]], axis=0)

    def rb_copies(ia, d):
        ib = rem(cb + d, NX)
        return [
            remote(codes.at[ia, ib], rb.at[d - 1, ia], rb_send.at[0, d - 1, ia], rb_recv.at[0, d - 1, ia], bdev(d)),
            remote(stats.at[ia, ib], rbs.at[d - 1, ia], rb_send.at[1, d - 1, ia], rb_recv.at[1, d - 1, ia], bdev(d)),
        ]

    def ra_copies(d):
        ia = rem(ca + d, NX)
        return [
            remote(codes2.at[ia], ra.at[d - 1], ra_send.at[0, d - 1], ra_recv.at[0, d - 1], adev(d)),
            remote(stats2.at[ia], ras.at[d - 1], ra_send.at[1, d - 1], ra_recv.at[1, d - 1], adev(d)),
        ]

    def rz_copies(d):
        rows = pl.ds(pl.multiple_of(rem(z + d, NZ) * SHARE, SHARE), SHARE)
        return [
            remote(codes3.at[:, rows, :], rz.at[d - 1], rz_send.at[0, d - 1], rz_recv.at[0, d - 1], zdev(d)),
            remote(stats3, rzs.at[d - 1], rz_send.at[1, d - 1], rz_recv.at[1, d - 1], zdev(d)),
        ]

    def reduce_b(delta):
        ia = rem(ca + delta, NX)
        for d in range(1, NX):
            for copy in rb_copies(ia, d):
                copy.wait_recv()

        def store(e, code):
            codes2[ia, e] = code

        stats2[ia] = blend_and_encode(
            [stats[ia, cb]] + [rbs[d, ia] for d in range(NX - 1)],
            lambda e: [codes[ia, cb, e]] + [rb[d, ia, e] for d in range(NX - 1)],
            store,
        )
        if delta:
            for copy in ra_copies(delta):
                copy.start()

    def reduce_a():
        for d in range(1, NX):
            for copy in ra_copies(d):
                copy.wait_recv()

        def store(e, code):
            codes3[e] = code

        stats3[...] = blend_and_encode(
            [stats2[ca]] + [ras[d] for d in range(NX - 1)],
            lambda e: [codes2[ca, e]] + [ra[d, e] for d in range(NX - 1)],
            store,
        )
        for d in (4, 3, 5, 2, 6, 1, 7):
            for copy in rz_copies(d):
                copy.start()

    def reduce_z():
        for d in range(1, NZ):
            for copy in rz_copies(d):
                copy.wait_recv()
        turned[...], unused = merge([stats3[...]] + [rzs[d] for d in range(NZ - 1)])
        rows = pl.ds(zrow, SHARE)
        coefficients = turned[rows, :]
        for e in range(GH):
            o = blend(coefficients, [codes3[e, rows, :]] + [rz[d, e] for d in range(NZ - 1)], e)
            suf_ref[:, e * HSZ : (e + 1) * HSZ] = o.astype(suf_ref.dtype)

    def q_b():
        for d in range(1, NX):
            bq_copy(rem(cb + NX - d, NX), d).wait_recv()
        for i in range(1, NX):
            for d in (2, 1, 3):
                aq_copy(ca, rem(cb + i, NX), d).start()

    def all_of(*steps):
        def run():
            for step, *arguments in steps:
                step(*arguments)

        return run

    q_b()
    kvs_copy.wait_recv()
    anchor_first(2)
    anchor_second(0)

    before = {
        1: all_of((anchor_second, 1)),
        2: all_of((anchor_second, 2)),
        4: all_of((anchor_z, 0)),
        5: all_of((anchor_z, 1)),
        6: all_of((anchor_b, 0)),
        7: all_of((anchor_z, 2)),
    }

    @pl.loop(0, NX * NY // 2)
    def _(n):
        for at, event in before.items():
            pl.when(n == at)(event)
        group, step, late = lax.div(n, 2), 2 * rem(n, 2), jnp.where(n < 4, 0, 3)
        delta = jnp.where(group < 2, group, 5 - group)
        deltas = (jnp.where(first, delta, late), jnp.where(first, delta, jnp.where(n < 4, 1, 2)))
        steps = (jnp.where(first, step, rem(n, 4)), jnp.where(first, step + 1, rem(n, 4)))
        blocks = [(rem(ca + delta, NX), rem(cb + step, NX)) for delta, step in zip(deltas, steps)]
        for delta, (ia, ib) in zip(deltas, blocks):

            @pl.when(delta > 0)
            def _():
                aq_copy(ia, ib, jnp.where(delta > 0, NX - delta, 1)).wait_recv()

        own_heads = jnp.where(first, *blocks[0]) == x

        @pl.when(own_heads)
        def _():
            suffix_pair(blocks, True)

        @pl.when(jnp.logical_not(own_heads))
        def _():
            suffix_pair(blocks, False)

        for step, (ia, ib) in zip(steps, blocks):

            @pl.when(step > 0)
            def _():
                for copy in rb_copies(ia, jnp.where(step > 0, step, 1)):
                    copy.start()

    anchor_b(1)
    reduce_b(1)
    reduce_b(3)
    anchor_b(2)
    anchor_a(0)
    reduce_b(2)

    def anchor_scores(h, t):
        q = q_v[t * TQ : (t + 1) * TQ, columns(h)]
        return lax.dot_general(q, anc[0, :, columns(h)], NT, preferred_element_type=jnp.float32) + abias[...]

    def anchor_finish(h, t, s):
        rows = slice(t * TQ, (t + 1) * TQ)
        before = m1[h, rows, :]
        m = jnp.maximum(before, jnp.max(s, axis=1, keepdims=True))
        p = jnp.exp2((s - wide(m, BLK // HSZ)) * SCALE2)
        fade = jnp.exp2((before - m) * SCALE2)
        l = l1[h, rows, :] * fade + jnp.sum(p, axis=1, keepdims=True)
        o = jnp.dot(p.astype(jnp.bfloat16), anc[1, :, columns(h)], preferred_element_type=jnp.float32)
        o = (acc1[h, rows, :] * fade + o) / l
        token = lax.broadcasted_iota(jnp.int32, (TQ, HSZ), 0) + t * TQ
        obuf[h, rows, :] = jnp.where(token < own_len, o, 0.0).astype(obuf.dtype)

    def out_copy(h):
        return pltpu.make_async_copy(obuf.at[h], ctx_hbm.at[:, columns(h)], out_sem.at[h])

    tail = {
        1: all_of((anchor_a, 1)),
        2: all_of((anchor_a, 2), (reduce_b, 0)),
        4: all_of((reduce_a,)),
    }

    @pl.loop(0, HEADS // 2)
    def _(t):
        for at, event in tail.items():
            pl.when(t == at)(event)
        k, other = lax.div(t, 2), rem(t, 2)

        @pl.when(other == 1)
        def _():
            sib_copy(k, 1 - c).wait_recv()

        h = rem(c + other, 2) * (HEADS // 2) + 2 * k
        pipelined([(h + i, tile) for i in range(2) for tile in range(BLK // TQ)], anchor_scores, anchor_finish)
        for i in range(2):
            out_copy(h + i).start()

    reduce_z()

    for copy in zq + [kvs_copy, sk_copy]:
        copy.wait_send()
    for d in range(1, NX):
        bq_copy(cb, d).wait_send()
        for pb in range(NX):
            aq_copy(ca, pb, d).wait_send()
        for copy in ra_copies(d):
            copy.wait_send()

    @pl.loop(0, NX)
    def _(ia):
        for d in range(1, NX):
            for copy in rb_copies(ia, d):
                copy.wait_send()

    @pl.loop(0, NCH)
    def _(k):
        for d in range(1, NX):
            bb_copy(k, cb, d).wait_send()
            ab_copy(k, ca, d).wait_send()
        sib_copy(k, c).wait_send()

        @pl.when(z == 0)
        def _():
            for d in range(1, NZ):
                zb_copy(k, d).wait_send()

        @pl.when((z == 0) & (cb == 0))
        def _():
            for d in range(1, NX):
                sb_copy(k, d).wait_send()

        @pl.when(is_root)
        def _():
            @pl.loop(1, 2 * NX)
            def _(i):
                scatter_copy(k, i).wait_send()

    for d in range(1, NZ):
        for copy in rz_copies(d):
            copy.wait_send()

    @pl.loop(0, HEADS)
    def _(h):
        out_copy(h).wait()


def per_device(queries, keys_values, token_ids, lengths, suffix_queries, suffix_kv):
    bf16, f32, i16 = jnp.bfloat16, jnp.float32, jnp.int16
    dma = pltpu.SemaphoreType.DMA
    scratch = [
        pltpu.VMEM((BLK, HD), bf16),
        pltpu.VMEM((2, BLK, HD), bf16),
        pltpu.VMEM((2, BLK, HD), bf16),
        pltpu.VMEM((3, 8, HSZ), jnp.int32),
        pltpu.VMEM((2, HSZ, GH * HSZ), bf16),
        pltpu.VMEM((NX, NX, GH, QB, HSZ), bf16),
        pltpu.VMEM((2, BLK, HD), bf16),
        pltpu.VMEM((NCH, 2, AROWS, CW), bf16),
        pltpu.VMEM((HEADS, BLK, HSZ), f32),
        pltpu.VMEM((HEADS, BLK, HSZ), f32),
        pltpu.VMEM((HEADS, BLK, HSZ), f32),
        pltpu.VMEM((BLK, BLK), f32),
        pltpu.VMEM((1, 2 * BLK), f32),
        pltpu.VMEM((1, BLK), f32),
        pltpu.VMEM((NX, NX, GH, QB, HSZ), i16),
        pltpu.VMEM((NX, NX, 8, HSZ), f32),
        pltpu.VMEM((NX - 1, NX, GH, QB, HSZ), i16),
        pltpu.VMEM((NX - 1, NX, 8, HSZ), f32),
        pltpu.VMEM((NX, GH, QB, HSZ), i16),
        pltpu.VMEM((NX, 8, HSZ), f32),
        pltpu.VMEM((NX - 1, GH, QB, HSZ), i16),
        pltpu.VMEM((NX - 1, 8, HSZ), f32),
        pltpu.VMEM((GH, QB, HSZ), i16),
        pltpu.VMEM((8, HSZ), f32),
        pltpu.VMEM((NZ - 1, GH, SHARE, HSZ), i16),
        pltpu.VMEM((NZ - 1, 8, HSZ), f32),
        pltpu.VMEM((HSZ, HSZ), f32),
        pltpu.VMEM((HEADS, BLK, HSZ), bf16),
        dma((9,)),
        dma, dma, dma, dma,
        dma((NZ - 1,)), dma((NZ - 1,)),
        dma((NX - 1,)), dma((NX - 1,)),
        dma((NX - 1, NX)), dma((NX - 1, NX)),
        dma((NCH, 2 * NX)), dma((NCH,)), dma((NCH,)),
        dma((NCH, NX - 1)), dma((NCH,)),
        dma((NCH, NZ - 1)), dma((NCH,)),
        dma((NCH, NX - 1)), dma((NCH, NX - 1)),
        dma((NCH, NX - 1)), dma((NCH, NX - 1)),
        dma((NCH,)), dma((NCH,)),
        dma((2, NX - 1, NX)), dma((2, NX - 1, NX)),
        dma((2, NX - 1)), dma((2, NX - 1)),
        dma((2, NZ - 1)), dma((2, NZ - 1)),
        dma((HEADS,)),
    ]
    anywhere = pl.BlockSpec(memory_space=pl.ANY)
    return pl.pallas_call(
        kernel,
        out_shape=(
            jax.ShapeDtypeStruct((BLK, HD), bf16),
            jax.ShapeDtypeStruct((SHARE, GH * HSZ), bf16),
        ),
        in_specs=[anywhere, anywhere, anywhere, pl.BlockSpec(memory_space=pltpu.SMEM), anywhere, anywhere],
        out_specs=(anywhere, pl.BlockSpec(memory_space=pltpu.VMEM)),
        scratch_shapes=scratch,
        compiler_params=pltpu.CompilerParams(
            collective_id=0, has_side_effects=True, vmem_limit_bytes=56 * 2**20
        ),
        cost_estimate=pl.CostEstimate(
            flops=6_500_000_000, bytes_accessed=6_500_000, transcendentals=12_600_000
        ),
        name="star",
    )(queries, keys_values, token_ids.reshape(-1, HSZ), lengths, suffix_queries, suffix_kv)


def solution(mesh):
    return jax.shard_map(
        per_device,
        mesh=mesh,
        in_specs=(
            P(("hst", "grp"), None),
            P(None, ("hst", "grp"), None),
            P(),
            P(),
            P("hst", "grp"),
            P(None, "hst", "grp"),
        ),
        out_specs=(P(("hst", "grp"), None), P("hst", "grp")),
        check_vma=False,
    )
```

```python
import math

import jax
import jax.numpy as jnp
from jax import lax
from jax.experimental import pallas as pl
from jax.experimental.pallas import tpu as pltpu
from jax.sharding import PartitionSpec as P

HEADS = 12
HSZ = 128
BLK = 512
HD = HEADS * HSZ
NAMB = 512
NEG = -1e30
FLOOR = -1e29
SCALE2 = math.log2(math.e) / math.sqrt(HSZ)
CODE = 32767.0
SIZES = (4, 4, 8)
NX, NY, NZ = SIZES
GH = HEADS // NX
SHARE = 16
QB = NZ * SHARE
TQ = 256
NCH = 3
CW = HD // 2 // NCH
PROWS = BLK // (NX * NY)
AROWS = BLK // NX
NT = (((1,), (1,)), ((), ()))
MESH = pl.DeviceIdType.MESH


def rem(a, n):
    return lax.rem(a, jnp.int32(n))


def kernel(
    q_hbm, kv_hbm, tok_hbm, lens, sq_hbm, skv_hbm,
    ctx_out, suf_out,
    q_v, kv_v, kvs, tok_v, ksuf, qbuf, anc, stage, acc1, m1, l1, own2d, bias, abias,
    codes, stats, rb, rbs, codes2, stats2, ra, ras, codes3, stats3, rz, rzs, turned, obuf, suf_v,
    in_sem, kvs_send, kvs_recv, sk_send, sk_recv,
    zq_send, zq_recv, bq_send, bq_recv, aq_send, aq_recv,
    sc_send, sc_recv, own_sem, sb_send, sb_recv, zb_send, zb_recv, bb_send, bb_recv, ab_send, ab_recv, sib_send, sib_recv,
    rb_send, rb_recv, ra_send, ra_recv, rz_send, rz_recv,
    out_sem, suf_sem,
):
    hst = lax.axis_index("hst")
    x = lax.axis_index("grp")
    c = rem(hst, 2)
    z = rem(lax.div(hst, 2), NZ)
    y = lax.div(hst, 2 * NZ)
    block = hst * NX + x
    first = c == 0
    ca = jnp.where(first, x, y)
    cb = jnp.where(first, y, x)

    def dev(px, py, pz, pc):
        return ((py * NZ + pz) * 2 + pc, px)

    def place(pa, pb, pz, pc):
        on = pc == 0
        return dev(jnp.where(on, pa, pb), jnp.where(on, pb, pa), pz, pc)

    def adev(delta):
        return place(rem(ca + delta, NX), cb, z, c)

    def bdev(delta):
        return place(ca, rem(cb + delta, NX), z, c)

    def zdev(delta):
        return dev(x, y, rem(z + delta, NZ), c)

    sibling = dev(x, y, z, 1 - c)

    def remote(src, dst, send, recv, to):
        return pltpu.make_async_remote_copy(
            src_ref=src, dst_ref=dst, send_sem=send, recv_sem=recv, device_id=to, device_id_type=MESH
        )

    def sent(ref, send):
        remote(ref, ref, send, kvs_recv, sibling).wait_send()

    def received(ref, recv):
        remote(ref, ref, kvs_send, recv, sibling).wait_recv()

    sblock = (hst + 1 - 2 * c) * NX + x
    zrow = pl.multiple_of(z * SHARE, SHARE)
    qloads = [
        pltpu.make_async_copy(
            sq_hbm.at[:, pl.ds(e * HSZ, HSZ)], qbuf.at[ca, cb, e, pl.ds(zrow, SHARE), :], in_sem.at[4]
        )
        for e in range(GH)
    ]
    loads = [
        pltpu.make_async_copy(q_hbm, q_v, in_sem.at[0]),
        pltpu.make_async_copy(kv_hbm, kv_v, in_sem.at[1]),
        pltpu.make_async_copy(skv_hbm, ksuf.at[:, pl.ds(0, SHARE), :], in_sem.at[2]),
    ]
    for i, b in enumerate((block, sblock, 0)):
        row = pl.multiple_of(lax.div(b, 2) * 8, 8)
        loads.append(pltpu.make_async_copy(tok_hbm.at[pl.ds(row, 8), :], tok_v.at[pl.ds(8 * i, 8), :], in_sem.at[3]))
    for copy in qloads + loads:
        copy.start()

    barrier = pltpu.get_barrier_semaphore()
    partners = [sibling]
    partners += [adev(d) for d in range(1, NX)] + [bdev(d) for d in range(1, NY)]
    partners += [zdev(d) for d in range(1, NZ)]
    for partner in partners:
        pl.semaphore_signal(barrier, inc=1, device_id=partner, device_id_type=MESH)
    is_root = block == 0
    is_extra = (z == 0) & (x == 0) & (y > 0) & (c == 1)

    @pl.when(is_extra)
    def _():
        pl.semaphore_signal(barrier, inc=1, device_id=(0, 0), device_id_type=MESH)

    pl.semaphore_wait(barrier, len(partners) + jnp.where(is_root, NY - 1, 0))

    ref = qbuf.at[ca, cb, :, pl.ds(zrow, SHARE), :]
    pltpu.make_async_copy(ref, ref, in_sem.at[4]).wait()
    zq = []
    for d in range(1, NZ):
        ref = qbuf.at[ca, cb, :, pl.ds(zrow, SHARE), :]
        zq.append(remote(ref, ref, zq_send, zq_recv, zdev(d)))
        zq[-1].start()

    kvs_copy = remote(kv_hbm, kvs, kvs_send, kvs_recv, sibling)
    kvs_copy.start()
    sk_copy = remote(skv_hbm, ksuf.at[:, pl.ds(SHARE, SHARE), :], sk_send, sk_recv, sibling)
    sk_copy.start()

    def piece(ref, k, pa, pb, core, rows):
        row = pl.multiple_of(pa * AROWS + pb * PROWS, PROWS)
        col = pl.multiple_of(core * (HD // 2) + k * CW, HSZ)
        return ref.at[:, pl.ds(row, rows), pl.ds(col, CW)]

    def scatter_copy(k, i):
        core, pa = rem(i, 2), lax.div(i, 2)
        src = piece(kv_hbm, k, pa, 0, core, AROWS)
        return remote(src, stage.at[k], sc_send, sc_recv.at[k], place(pa, 0, 0, core))

    def root_own(k):
        return pltpu.make_async_copy(piece(kv_hbm, k, 0, 0, 0, AROWS), stage.at[k], own_sem.at[k])

    @pl.when(is_root)
    def _():
        for k in range(NCH):
            root_own(k).start()
            for i in (4, 5, 2, 3, 6, 7, 1):
                scatter_copy(k, jnp.int32(i)).start()

    def sb_copy(k, d):
        src = stage.at[k, :, pl.ds(d * PROWS, PROWS), :]
        return remote(src, piece(anc, k, ca, rem(cb + d, NX), c, PROWS), sb_send, sb_recv.at[k], bdev(d))

    def zb_copy(k, d):
        ref = piece(anc, k, ca, cb, c, PROWS)
        return remote(ref, ref, zb_send, zb_recv.at[k], zdev(d))

    def bb_copy(k, pb, d):
        ref = piece(anc, k, ca, pb, c, PROWS)
        return remote(ref, ref, bb_send, bb_recv.at[k], bdev(d))

    def ab_copy(k, pa, d):
        ref = piece(anc, k, pa, 0, c, AROWS)
        return remote(ref, ref, ab_send, ab_recv.at[k], adev(d))

    def sib_copy(k, core):
        ref = piece(anc, k, 0, 0, core, BLK)
        return remote(ref, ref, sib_send, sib_recv.at[k], sibling)

    def anchor_first(k):
        @pl.when((z == 0) & (cb == 0))
        def _():
            @pl.when(is_root)
            def _():
                root_own(k).wait()

            @pl.when(jnp.logical_not(is_root))
            def _():
                remote(stage.at[k], stage.at[k], sib_send, sc_recv.at[k], sibling).wait_recv()

            for d in (2, 1, 3):
                sb_copy(k, d).start()
            row = pl.multiple_of(ca * AROWS, AROWS)
            col = pl.multiple_of(c * (HD // 2) + k * CW, HSZ)
            anc[:, pl.ds(row, PROWS), pl.ds(col, CW)] = stage[k, :, 0:PROWS, :]

    def anchor_second(k):
        @pl.when(z == 0)
        def _():
            @pl.when(cb > 0)
            def _():
                ref = piece(anc, k, ca, cb, c, PROWS)
                remote(ref, ref, sib_send, sb_recv.at[k], sibling).wait_recv()

            for d in (4, 3, 5, 2, 6, 1, 7):
                zb_copy(k, d).start()

    def anchor_z(k):
        @pl.when(z > 0)
        def _():
            zb_copy(k, 1).wait_recv()

        for d in (2, 1, 3):
            bb_copy(k, cb, d).start()

    def anchor_b(k):
        received(anc.at[:, pl.ds(0, (NX - 1) * PROWS), pl.ds(0, CW)], bb_recv.at[k])
        for d in (2, 1, 3):
            ab_copy(k, ca, d).start()

    def anchor_a(k):
        received(anc.at[:, pl.ds(0, (NX - 1) * AROWS), pl.ds(0, CW)], ab_recv.at[k])
        sib_copy(k, c).start()

    pltpu.make_async_copy(tok_hbm.at[pl.ds(0, 24), :], tok_v, in_sem.at[3]).wait()
    flat = lax.broadcasted_iota(jnp.int32, (4, HSZ), 0) * HSZ + lax.broadcasted_iota(jnp.int32, (4, HSZ), 1)

    def key_bias(i, b, length, on):
        both = tok_v[8 * i : 8 * i + 8]
        ids = jnp.where(rem(b, 2) == 1, both[4:8], both[0:4])
        part = jnp.where((ids >= NAMB) & (flat < length) & on, 0.0, NEG)
        return jnp.concatenate([part[r : r + 1] for r in range(4)], axis=1)

    own_len = lens[block]
    own_bias = key_bias(0, block, own_len, True)
    bias[:, 0:BLK] = own_bias
    bias[:, BLK:] = key_bias(1, sblock, lens[sblock], True)
    abias[...] = key_bias(2, jnp.int32(0), lens[0], block > 0)
    row2d = lax.broadcasted_iota(jnp.int32, (BLK, BLK), 0)
    col2d = lax.broadcasted_iota(jnp.int32, (BLK, BLK), 1)
    own2d[...] = jnp.where(col2d == row2d, 0.0, jnp.where(col2d < row2d, own_bias, NEG))
    ksuf[:, 2 * SHARE :, :] = jnp.zeros((2, HSZ - 2 * SHARE, GH * HSZ), ksuf.dtype)

    def columns(h):
        return pl.ds(pl.multiple_of(h * HSZ, HSZ), HSZ)

    def wide(a, copies):
        return jnp.concatenate([a] * copies, axis=1)

    def pipelined(units, scores, finish):
        ready = scores(*units[0])
        for i, unit in enumerate(units):
            later = scores(*units[i + 1]) if i + 1 < len(units) else None
            finish(*unit, ready)
            ready = later

    loads[0].wait()
    loads[1].wait()

    def own_scores(h, t):
        q = q_v[t * TQ : (t + 1) * TQ, columns(h)]
        k = kv_v[0, 0 : (t + 1) * TQ, columns(h)]
        s = lax.dot_general(q, k, NT, preferred_element_type=jnp.float32)
        return s + own2d[t * TQ : (t + 1) * TQ, 0 : (t + 1) * TQ]

    def own_finish(h, t, s):
        rows = slice(t * TQ, (t + 1) * TQ)
        m = jnp.max(s, axis=1, keepdims=True)
        p = jnp.exp2((s - m) * SCALE2)
        v = kv_v[1, 0 : (t + 1) * TQ, columns(h)]
        l1[h, rows, :] = jnp.broadcast_to(jnp.sum(p, axis=1, keepdims=True), (TQ, HSZ))
        m1[h, rows, :] = jnp.broadcast_to(m, (TQ, HSZ))
        acc1[h, rows, :] = jnp.dot(p.astype(jnp.bfloat16), v, preferred_element_type=jnp.float32)

    @pl.loop(0, HEADS // 2)
    def _(t):
        pipelined([(2 * t + i, tile) for i in range(2) for tile in range(BLK // TQ)], own_scores, own_finish)

    def bq_copy(pb, d):
        ref = qbuf.at[ca, pb]
        return remote(ref, ref, bq_send, bq_recv, bdev(d))

    def aq_copy(pa, pb, d):
        ref = qbuf.at[pa, pb]
        return remote(ref, ref, aq_send, aq_recv.at[d - 1, pb], adev(d))

    received(qbuf.at[0, 0, :, pl.ds(0, (NZ - 1) * SHARE), :], zq_recv)
    for d in (2, 1, 3):
        bq_copy(cb, d).start()
    for d in (2, 1, 3):
        aq_copy(ca, cb, d).start()
    anchor_first(0)
    anchor_first(1)

    sk_copy.wait_recv()
    loads[2].wait()
    lane = lax.broadcasted_iota(jnp.int32, (QB, HSZ), 1)
    pair_lane = lax.broadcasted_iota(jnp.int32, (2 * QB, HSZ), 1)
    pair_row = lax.broadcasted_iota(jnp.int32, (2 * QB, HSZ), 0)

    def encode(o):
        a = jnp.maximum(jnp.max(jnp.abs(o), axis=-1, keepdims=True), 1e-30)
        return a, jnp.round(o * (CODE / a)).astype(jnp.int32).astype(jnp.int16)

    def suffix_pair(blocks, with_suffix):
        bx = jnp.where(first, *blocks[0])
        bys = [jnp.where(first, ib, ia) for ia, ib in blocks]

        def scores(e):
            q = jnp.concatenate([qbuf[ia, ib, e] for ia, ib in blocks], axis=0)
            parts = []
            for i, ref in enumerate((kv_v, kvs)):
                s = lax.dot_general(q, ref[0, :, columns(GH * bx + e)], NT, preferred_element_type=jnp.float32)
                parts.append(s + bias[:, i * BLK : (i + 1) * BLK])
            if with_suffix:
                by = jnp.where(pair_row < QB, bys[0], bys[1] - 1)
                qpos = by * (2 * QB) + lax.div(pair_row, SHARE) * (2 * SHARE) + c * SHARE + rem(pair_row, SHARE)
                other = (hst + 1 - 2 * c) * SHARE + pair_lane - SHARE
                kpos = jnp.where(pair_lane < SHARE, hst * SHARE + pair_lane, other)
                s = lax.dot_general(q, ksuf[0, :, e * HSZ : (e + 1) * HSZ], NT, preferred_element_type=jnp.float32)
                parts.append(jnp.where((pair_lane < 2 * SHARE) & (kpos <= qpos), s, NEG))
            return jnp.concatenate(parts, axis=1)

        columns_of = []

        def finish(e, s):
            m = jnp.maximum(jnp.max(s, axis=1, keepdims=True), FLOOR)
            p = jnp.exp2((s - m) * SCALE2)
            l = jnp.maximum(jnp.sum(p, axis=1, keepdims=True), 1.0)
            w = p.astype(jnp.bfloat16)
            h = GH * bx + e
            o = jnp.dot(w[:, :BLK], kv_v[1, :, columns(h)], preferred_element_type=jnp.float32)
            o = o + jnp.dot(w[:, BLK : 2 * BLK], kvs[1, :, columns(h)], preferred_element_type=jnp.float32)
            if with_suffix:
                v = ksuf[1, :, e * HSZ : (e + 1) * HSZ]
                o = o + jnp.dot(w[:, 2 * BLK :], v, preferred_element_type=jnp.float32)
            a, code = encode(o / l)
            lse = m * SCALE2 + jnp.log2(l)
            for i, (ia, ib) in enumerate(blocks):
                codes[ia, ib, e] = code[i * QB : (i + 1) * QB]
            columns_of.append((lse, a))

        pipelined([(e,) for e in range(GH)], scores, finish)
        for i, (ia, ib) in enumerate(blocks):
            rows = slice(i * QB, (i + 1) * QB)
            stats[ia, ib] = rows_of([(lse[rows], a[rows]) for lse, a in columns_of])

    def rows_of(columns_of):
        flat_stats = jnp.zeros((QB, HSZ), jnp.float32)
        for e, (lse, a) in enumerate(columns_of):
            flat_stats = jnp.where(lane == e, lse, jnp.where(lane == 4 + e, a, flat_stats))
        return flat_stats.T[0:8]

    def merge(parts):
        lses = [s[0:4] for s in parts]
        top = lses[0]
        for s in lses[1:]:
            top = jnp.maximum(top, s)
        weights = [jnp.exp2(s - top) for s in lses]
        total = weights[0]
        for w in weights[1:]:
            total = total + w
        inverse = 1.0 / (total * CODE)
        rows = jnp.concatenate([w * inverse * s[4:8] for w, s in zip(weights, parts)], axis=0)
        rows = jnp.concatenate([rows, jnp.zeros((HSZ - rows.shape[0], HSZ), jnp.float32)], axis=0)
        return rows.T, top + jnp.log2(total)

    def blend(coefficients, coded, e):
        total = None
        for i, code in enumerate(coded):
            term = coefficients[:, 4 * i + e : 4 * i + e + 1] * code.astype(jnp.int32).astype(jnp.float32)
            total = term if total is None else total + term
        return total

    def blend_and_encode(parts, coded_of, store):
        coefficients, lse = merge(parts)
        scales = []
        for e in range(GH):
            a, code = encode(blend(coefficients, coded_of(e), e))
            store(e, code)
            scales.append((a, a))
        return jnp.concatenate([lse, rows_of(scales)[0:4]], axis=0)

    def rb_copies(ia, d):
        ib = rem(cb + d, NX)
        return [
            remote(codes.at[ia, ib], rb.at[d - 1, ia], rb_send.at[0], rb_recv.at[0, ia], bdev(d)),
            remote(stats.at[ia, ib], rbs.at[d - 1, ia], rb_send.at[1], rb_recv.at[1, ia], bdev(d)),
        ]

    def ra_copies(d):
        ia = rem(ca + d, NX)
        return [
            remote(codes2.at[ia], ra.at[d - 1], ra_send.at[0], ra_recv.at[0], adev(d)),
            remote(stats2.at[ia], ras.at[d - 1], ra_send.at[1], ra_recv.at[1], adev(d)),
        ]

    def rz_copies(d):
        rows = pl.ds(pl.multiple_of(rem(z + d, NZ) * SHARE, SHARE), SHARE)
        return [
            remote(codes3.at[:, rows, :], rz.at[d - 1], rz_send.at[0], rz_recv.at[0], zdev(d)),
            remote(stats3, rzs.at[d - 1], rz_send.at[1], rz_recv.at[1], zdev(d)),
        ]

    def reduce_b(delta):
        ia = rem(ca + delta, NX)
        received(rb.at[:, ia], rb_recv.at[0, ia])
        received(rbs.at[:, ia], rb_recv.at[1, ia])

        def store(e, code):
            codes2[ia, e] = code

        stats2[ia] = blend_and_encode(
            [stats[ia, cb]] + [rbs[d, ia] for d in range(NX - 1)],
            lambda e: [codes[ia, cb, e]] + [rb[d, ia, e] for d in range(NX - 1)],
            store,
        )
        if delta:
            for copy in ra_copies(delta):
                copy.start()

    def reduce_a():
        received(ra, ra_recv.at[0])
        received(ras, ra_recv.at[1])

        def store(e, code):
            codes3[e] = code

        stats3[...] = blend_and_encode(
            [stats2[ca]] + [ras[d] for d in range(NX - 1)],
            lambda e: [codes2[ca, e]] + [ra[d, e] for d in range(NX - 1)],
            store,
        )
        for d in (4, 3, 5, 2, 6, 1, 7):
            for copy in rz_copies(d):
                copy.start()

    def reduce_z():
        received(rz, rz_recv.at[0])
        received(rzs, rz_recv.at[1])
        turned[...], unused = merge([stats3[...]] + [rzs[d] for d in range(NZ - 1)])
        rows = pl.ds(zrow, SHARE)
        coefficients = turned[rows, :]
        for e in range(GH):
            o = blend(coefficients, [codes3[e, rows, :]] + [rz[d, e] for d in range(NZ - 1)], e)
            suf_v[:, e * HSZ : (e + 1) * HSZ] = o.astype(suf_v.dtype)
        pltpu.make_async_copy(suf_v, suf_out, suf_sem).start()

    def q_b():
        received(qbuf.at[0, pl.ds(0, NX - 1)], bq_recv)
        for i in range(1, NX):
            for d in (2, 1, 3):
                aq_copy(ca, rem(cb + i, NX), d).start()

    def all_of(*steps):
        def run():
            for step, *arguments in steps:
                step(*arguments)

        return run

    q_b()
    kvs_copy.wait_recv()
    anchor_first(2)
    anchor_second(0)

    before = {
        0: all_of((anchor_second, 1)),
        1: all_of((anchor_second, 2)),
        3: all_of((anchor_z, 0)),
        4: all_of((anchor_z, 1)),
        5: all_of((anchor_z, 2), (anchor_b, 0)),
        6: all_of((anchor_b, 1)),
        7: all_of((anchor_b, 2), (reduce_b, 1)),
    }

    @pl.loop(0, NX * NY // 2)
    def _(n):
        for at, event in before.items():
            pl.when(n == at)(event)
        group, step, late = lax.div(n, 2), 2 * rem(n, 2), jnp.where(n < 4, 0, 3)
        delta = jnp.where(group < 2, group, 5 - group)
        deltas = (jnp.where(first, delta, late), jnp.where(first, delta, jnp.where(n < 4, 1, 2)))
        steps = (jnp.where(first, step, rem(n, 4)), jnp.where(first, step + 1, rem(n, 4)))
        blocks = [(rem(ca + delta, NX), rem(cb + step, NX)) for delta, step in zip(deltas, steps)]
        for delta, (ia, ib) in zip(deltas, blocks):

            @pl.when(delta > 0)
            def _():
                aq_copy(ia, ib, jnp.where(delta > 0, NX - delta, 1)).wait_recv()

        own_heads = jnp.where(first, *blocks[0]) == x

        @pl.when(own_heads)
        def _():
            suffix_pair(blocks, True)

        @pl.when(jnp.logical_not(own_heads))
        def _():
            suffix_pair(blocks, False)

        for step, (ia, ib) in zip(steps, blocks):

            @pl.when(step > 0)
            def _():
                for copy in rb_copies(ia, jnp.where(step > 0, step, 1)):
                    copy.start()

    anchor_a(0)
    reduce_b(0)
    reduce_b(3)

    def anchor_scores(h, t):
        q = q_v[t * TQ : (t + 1) * TQ, columns(h)]
        return lax.dot_general(q, anc[0, :, columns(h)], NT, preferred_element_type=jnp.float32) + abias[...]

    def anchor_finish(h, t, s):
        rows = slice(t * TQ, (t + 1) * TQ)
        before = m1[h, rows, :]
        m = jnp.maximum(before, jnp.max(s, axis=1, keepdims=True))
        p = jnp.exp2((s - wide(m, BLK // HSZ)) * SCALE2)
        fade = jnp.exp2((before - m) * SCALE2)
        l = l1[h, rows, :] * fade + jnp.sum(p, axis=1, keepdims=True)
        o = jnp.dot(p.astype(jnp.bfloat16), anc[1, :, columns(h)], preferred_element_type=jnp.float32)
        o = (acc1[h, rows, :] * fade + o) / l
        token = lax.broadcasted_iota(jnp.int32, (TQ, HSZ), 0) + t * TQ
        obuf[h, rows, :] = jnp.where(token < own_len, o, 0.0).astype(obuf.dtype)

    def out_copy(h):
        return pltpu.make_async_copy(obuf.at[h], ctx_out.at[:, columns(h)], out_sem)

    tail = {
        1: all_of((anchor_a, 1), (reduce_b, 2)),
        2: all_of((anchor_a, 2)),
        4: all_of((reduce_a,)),
    }

    @pl.loop(0, HEADS // 2)
    def _(t):
        for at, event in tail.items():
            pl.when(t == at)(event)
        k, other = lax.div(t, 2), rem(t, 2)

        @pl.when(other == 1)
        def _():
            sib_copy(k, 1 - c).wait_recv()

        h = rem(c + other, 2) * (HEADS // 2) + 2 * k
        pipelined([(h + i, tile) for i in range(2) for tile in range(BLK // TQ)], anchor_scores, anchor_finish)
        for i in range(2):
            out_copy(h + i).start()

    reduce_z()

    for copy in (kvs_copy, sk_copy):
        copy.wait_send()
    sent(qbuf.at[0, 0, :, pl.ds(0, (NZ - 1) * SHARE), :], zq_send)
    sent(qbuf.at[0, pl.ds(0, NX - 1)], bq_send)
    sent(qbuf.at[pl.ds(0, NX - 1)], aq_send)
    sent(codes.at[pl.ds(0, NX - 1)], rb_send.at[0])
    sent(stats.at[pl.ds(0, NX - 1)], rb_send.at[1])
    sent(ra, ra_send.at[0])
    sent(ras, ra_send.at[1])
    sent(rz, rz_send.at[0])
    sent(rzs, rz_send.at[1])
    half = pl.ds(0, HD // 2)
    sent(anc.at[:, pl.ds(0, (NX - 1) * PROWS), half], bb_send)
    sent(anc.at[:, pl.ds(0, (NX - 1) * AROWS), half], ab_send)
    sent(anc.at[:, :, half], sib_send)

    @pl.when(z == 0)
    def _():
        sent(anc.at[:, pl.ds(0, (NZ - 1) * PROWS // 2), :], zb_send)

        @pl.when(cb == 0)
        def _():
            sent(anc.at[:, pl.ds(0, (NX - 1) * PROWS), half], sb_send)

    @pl.when(is_root)
    def _():
        sent(kv_v.at[:, pl.ds(0, (2 * NX - 1) * AROWS // 2), :], sc_send)

    pltpu.make_async_copy(suf_v, suf_out, suf_sem).wait()
    pltpu.make_async_copy(q_v, ctx_out, out_sem).wait()


def per_device(queries, keys_values, token_ids, lengths, suffix_queries, suffix_kv):
    bf16, f32, i16 = jnp.bfloat16, jnp.float32, jnp.int16
    dma = pltpu.SemaphoreType.DMA
    scratch = [
        pltpu.VMEM((BLK, HD), bf16),
        pltpu.VMEM((2, BLK, HD), bf16),
        pltpu.VMEM((2, BLK, HD), bf16),
        pltpu.VMEM((24, HSZ), jnp.int32),
        pltpu.VMEM((2, HSZ, GH * HSZ), bf16),
        pltpu.VMEM((NX, NX, GH, QB, HSZ), bf16),
        pltpu.VMEM((2, BLK, HD), bf16),
        pltpu.VMEM((NCH, 2, AROWS, CW), bf16),
        pltpu.VMEM((HEADS, BLK, HSZ), f32),
        pltpu.VMEM((HEADS, BLK, HSZ), f32),
        pltpu.VMEM((HEADS, BLK, HSZ), f32),
        pltpu.VMEM((BLK, BLK), f32),
        pltpu.VMEM((1, 2 * BLK), f32),
        pltpu.VMEM((1, BLK), f32),
        pltpu.VMEM((NX, NX, GH, QB, HSZ), i16),
        pltpu.VMEM((NX, NX, 8, HSZ), f32),
        pltpu.VMEM((NX - 1, NX, GH, QB, HSZ), i16),
        pltpu.VMEM((NX - 1, NX, 8, HSZ), f32),
        pltpu.VMEM((NX, GH, QB, HSZ), i16),
        pltpu.VMEM((NX, 8, HSZ), f32),
        pltpu.VMEM((NX - 1, GH, QB, HSZ), i16),
        pltpu.VMEM((NX - 1, 8, HSZ), f32),
        pltpu.VMEM((GH, QB, HSZ), i16),
        pltpu.VMEM((8, HSZ), f32),
        pltpu.VMEM((NZ - 1, GH, SHARE, HSZ), i16),
        pltpu.VMEM((NZ - 1, 8, HSZ), f32),
        pltpu.VMEM((HSZ, HSZ), f32),
        pltpu.VMEM((HEADS, BLK, HSZ), bf16),
        pltpu.VMEM((SHARE, GH * HSZ), bf16),
        dma((5,)),
        dma, dma, dma, dma,
        dma, dma,
        dma, dma,
        dma, dma((NX - 1, NX)),
        dma, dma((NCH,)), dma((NCH,)),
        dma, dma((NCH,)),
        dma, dma((NCH,)),
        dma, dma((NCH,)),
        dma, dma((NCH,)),
        dma, dma((NCH,)),
        dma((2,)), dma((2, NX)),
        dma((2,)), dma((2,)),
        dma((2,)), dma((2,)),
        dma, dma,
    ]
    anywhere = pl.BlockSpec(memory_space=pl.ANY)
    return pl.pallas_call(
        kernel,
        out_shape=(
            pltpu.VMEM((BLK, HD), bf16),
            pltpu.VMEM((SHARE, GH * HSZ), bf16),
        ),
        in_specs=[anywhere, anywhere, anywhere, pl.BlockSpec(memory_space=pltpu.SMEM), anywhere, anywhere],
        out_specs=(anywhere, anywhere),
        scratch_shapes=scratch,
        compiler_params=pltpu.CompilerParams(
            collective_id=0, has_side_effects=True, vmem_limit_bytes=56 * 2**20
        ),
        cost_estimate=pl.CostEstimate(
            flops=6_500_000_000, bytes_accessed=6_500_000, transcendentals=12_600_000
        ),
        name="star",
    )(queries, keys_values, token_ids.reshape(-1, HSZ), lengths, suffix_queries, suffix_kv)


def solution(mesh):
    return jax.shard_map(
        per_device,
        mesh=mesh,
        in_specs=(
            P(("hst", "grp"), None),
            P(None, ("hst", "grp"), None),
            P(),
            P(),
            P("hst", "grp"),
            P(None, "hst", "grp"),
        ),
        out_specs=(P(("hst", "grp"), None), P("hst", "grp")),
        check_vma=False,
    )
```

```python
import math

import jax
import jax.numpy as jnp
from jax import lax
from jax.experimental import pallas as pl
from jax.experimental.pallas import tpu as pltpu
from jax.sharding import PartitionSpec as P

HEADS = 12
HSZ = 128
BLK = 512
HD = HEADS * HSZ
NAMB = 512
NEG = -1e30
FLOOR = -1e29
SCALE2 = math.log2(math.e) / math.sqrt(HSZ)
CODE = 32767.0
SIZES = (4, 4, 8)
NX, NY, NZ = SIZES
GH = HEADS // NX
SHARE = 16
QB = NZ * SHARE
TQ = 256
NCH = 3
CW = HD // 2 // NCH
PROWS = BLK // (NX * NY)
AROWS = BLK // NX
NT = (((1,), (1,)), ((), ()))
MESH = pl.DeviceIdType.MESH


def rem(a, n):
    return lax.rem(a, jnp.int32(n))


def kernel(
    q_hbm, kv_hbm, tok_hbm, lens, sq_hbm, skv_hbm,
    ctx_out, suf_out,
    q_v, kv_v, kvs, tok_v, ksuf, qbuf, anc, stage, acc1, m1, l1, own2d, bias, abias,
    codes, stats, rb, rbs, codes2, stats2, ra, ras, codes3, stats3, rz, rzs, turned, obuf, suf_v,
    in_sem, kvs_send, kvs_recv, sk_send, sk_recv,
    zq_send, zq_recv, bq_send, bq_recv, aq_send, aq_recv,
    sc_send, sc_recv, own_sem, sb_send, sb_recv, zb_send, zb_recv, bb_send, bb_recv, ab_send, ab_recv, sib_send, sib_recv,
    rb_send, rb_recv, ra_send, ra_recv, rz_send, rz_recv,
    out_sem, suf_sem,
):
    hst = lax.axis_index("hst")
    x = lax.axis_index("grp")
    c = rem(hst, 2)
    z = rem(lax.div(hst, 2), NZ)
    y = lax.div(hst, 2 * NZ)
    block = hst * NX + x
    first = c == 0
    ca = jnp.where(first, x, y)
    cb = jnp.where(first, y, x)

    def dev(px, py, pz, pc):
        return ((py * NZ + pz) * 2 + pc, px)

    def place(pa, pb, pz, pc):
        on = pc == 0
        return dev(jnp.where(on, pa, pb), jnp.where(on, pb, pa), pz, pc)

    def adev(delta):
        return place(rem(ca + delta, NX), cb, z, c)

    def bdev(delta):
        return place(ca, rem(cb + delta, NX), z, c)

    def zdev(delta):
        return dev(x, y, rem(z + delta, NZ), c)

    sibling = dev(x, y, z, 1 - c)

    def remote(src, dst, send, recv, to):
        return pltpu.make_async_remote_copy(
            src_ref=src, dst_ref=dst, send_sem=send, recv_sem=recv, device_id=to, device_id_type=MESH
        )

    def sent(ref, send):
        remote(ref, ref, send, kvs_recv, sibling).wait_send()

    def received(ref, recv):
        remote(ref, ref, kvs_send, recv, sibling).wait_recv()

    sblock = (hst + 1 - 2 * c) * NX + x
    zrow = pl.multiple_of(z * SHARE, SHARE)
    qloads = [
        pltpu.make_async_copy(
            sq_hbm.at[:, pl.ds(e * HSZ, HSZ)], qbuf.at[ca, cb, e, pl.ds(zrow, SHARE), :], in_sem.at[4]
        )
        for e in range(GH)
    ]
    loads = [
        pltpu.make_async_copy(q_hbm, q_v, in_sem.at[0]),
        pltpu.make_async_copy(kv_hbm, kv_v, in_sem.at[1]),
        pltpu.make_async_copy(skv_hbm, ksuf.at[:, pl.ds(0, SHARE), :], in_sem.at[2]),
    ]
    for i, b in enumerate((block, sblock, 0)):
        row = pl.multiple_of(lax.div(b, 2) * 8, 8)
        loads.append(pltpu.make_async_copy(tok_hbm.at[pl.ds(row, 8), :], tok_v.at[pl.ds(8 * i, 8), :], in_sem.at[3]))
    for copy in qloads + loads:
        copy.start()

    barrier = pltpu.get_barrier_semaphore()
    partners = [sibling]
    partners += [adev(d) for d in range(1, NX)] + [bdev(d) for d in range(1, NY)]
    partners += [zdev(d) for d in range(1, NZ)]
    for partner in partners:
        pl.semaphore_signal(barrier, inc=1, device_id=partner, device_id_type=MESH)
    is_root = block == 0
    is_extra = (z == 0) & (x == 0) & (y > 0) & (c == 1)

    @pl.when(is_extra)
    def _():
        pl.semaphore_signal(barrier, inc=1, device_id=(0, 0), device_id_type=MESH)

    pl.semaphore_wait(barrier, len(partners) + jnp.where(is_root, NY - 1, 0))

    ref = qbuf.at[ca, cb, :, pl.ds(zrow, SHARE), :]
    pltpu.make_async_copy(ref, ref, in_sem.at[4]).wait()
    zq = []
    for d in range(1, NZ):
        ref = qbuf.at[ca, cb, :, pl.ds(zrow, SHARE), :]
        zq.append(remote(ref, ref, zq_send, zq_recv, zdev(d)))
        zq[-1].start()

    kvs_copy = remote(kv_hbm, kvs, kvs_send, kvs_recv, sibling)
    kvs_copy.start()
    sk_copy = remote(skv_hbm, ksuf.at[:, pl.ds(SHARE, SHARE), :], sk_send, sk_recv, sibling)
    sk_copy.start()

    def piece(ref, k, pa, pb, core, rows):
        row = pl.multiple_of(pa * AROWS + pb * PROWS, PROWS)
        col = pl.multiple_of(core * (HD // 2) + k * CW, HSZ)
        return ref.at[:, pl.ds(row, rows), pl.ds(col, CW)]

    def scatter_copy(k, i):
        core, pa = rem(i, 2), lax.div(i, 2)
        src = piece(kv_hbm, k, pa, 0, core, AROWS)
        return remote(src, stage.at[k], sc_send, sc_recv.at[k], place(pa, 0, 0, core))

    def root_own(k):
        return pltpu.make_async_copy(piece(kv_hbm, k, 0, 0, 0, AROWS), stage.at[k], own_sem.at[k])

    @pl.when(is_root)
    def _():
        for k in range(NCH):
            root_own(k).start()
            for i in (4, 5, 2, 3, 6, 7, 1):
                scatter_copy(k, jnp.int32(i)).start()

    def sb_copy(k, d):
        src = stage.at[k, :, pl.ds(d * PROWS, PROWS), :]
        return remote(src, piece(anc, k, ca, rem(cb + d, NX), c, PROWS), sb_send, sb_recv.at[k], bdev(d))

    def zb_copy(k, d):
        ref = piece(anc, k, ca, cb, c, PROWS)
        return remote(ref, ref, zb_send, zb_recv.at[k], zdev(d))

    def bb_copy(k, pb, d):
        ref = piece(anc, k, ca, pb, c, PROWS)
        return remote(ref, ref, bb_send, bb_recv.at[k], bdev(d))

    def ab_copy(k, pa, d):
        ref = piece(anc, k, pa, 0, c, AROWS)
        return remote(ref, ref, ab_send, ab_recv.at[k], adev(d))

    def sib_copy(k, core):
        ref = piece(anc, k, 0, 0, core, BLK)
        return remote(ref, ref, sib_send, sib_recv.at[k], sibling)

    def anchor_first(k):
        @pl.when((z == 0) & (cb == 0))
        def _():
            @pl.when(is_root)
            def _():
                root_own(k).wait()

            @pl.when(jnp.logical_not(is_root))
            def _():
                remote(stage.at[k], stage.at[k], sib_send, sc_recv.at[k], sibling).wait_recv()

            for d in (2, 1, 3):
                sb_copy(k, d).start()
            row = pl.multiple_of(ca * AROWS, AROWS)
            col = pl.multiple_of(c * (HD // 2) + k * CW, HSZ)
            anc[:, pl.ds(row, PROWS), pl.ds(col, CW)] = stage[k, :, 0:PROWS, :]

    def anchor_second(k):
        @pl.when(z == 0)
        def _():
            @pl.when(cb > 0)
            def _():
                ref = piece(anc, k, ca, cb, c, PROWS)
                remote(ref, ref, sib_send, sb_recv.at[k], sibling).wait_recv()

            for d in (4, 3, 5, 2, 6, 1, 7):
                zb_copy(k, d).start()

    def anchor_z(k):
        @pl.when(z > 0)
        def _():
            zb_copy(k, 1).wait_recv()

        for d in (2, 1, 3):
            bb_copy(k, cb, d).start()

    def anchor_b(k):
        received(anc.at[:, pl.ds(0, (NX - 1) * PROWS), pl.ds(0, CW)], bb_recv.at[k])
        for d in (2, 1, 3):
            ab_copy(k, ca, d).start()

    def anchor_a(k):
        received(anc.at[:, pl.ds(0, (NX - 1) * AROWS), pl.ds(0, CW)], ab_recv.at[k])
        sib_copy(k, c).start()

    pltpu.make_async_copy(tok_hbm.at[pl.ds(0, 24), :], tok_v, in_sem.at[3]).wait()
    flat = lax.broadcasted_iota(jnp.int32, (4, HSZ), 0) * HSZ + lax.broadcasted_iota(jnp.int32, (4, HSZ), 1)

    def key_bias(i, b, length, on):
        both = tok_v[8 * i : 8 * i + 8]
        ids = jnp.where(rem(b, 2) == 1, both[4:8], both[0:4])
        part = jnp.where((ids >= NAMB) & (flat < length) & on, 0.0, NEG)
        return jnp.concatenate([part[r : r + 1] for r in range(4)], axis=1)

    own_len = lens[block]
    own_bias = key_bias(0, block, own_len, True)
    bias[:, 0:BLK] = own_bias
    bias[:, BLK:] = key_bias(1, sblock, lens[sblock], True)
    abias[...] = key_bias(2, jnp.int32(0), lens[0], block > 0)
    row2d = lax.broadcasted_iota(jnp.int32, (BLK, BLK), 0)
    col2d = lax.broadcasted_iota(jnp.int32, (BLK, BLK), 1)
    own2d[...] = jnp.where(col2d == row2d, 0.0, jnp.where(col2d < row2d, own_bias, NEG))
    ksuf[:, 2 * SHARE :, :] = jnp.zeros((2, HSZ - 2 * SHARE, GH * HSZ), ksuf.dtype)

    def columns(h):
        return pl.ds(pl.multiple_of(h * HSZ, HSZ), HSZ)

    def wide(a, copies):
        return jnp.concatenate([a] * copies, axis=1)

    def pipelined(units, scores, finish):
        ready = scores(*units[0])
        for i, unit in enumerate(units):
            later = scores(*units[i + 1]) if i + 1 < len(units) else None
            finish(*unit, ready)
            ready = later

    loads[0].wait()
    loads[1].wait()

    def own_scores(h, t):
        q = q_v[t * TQ : (t + 1) * TQ, columns(h)]
        k = kv_v[0, 0 : (t + 1) * TQ, columns(h)]
        s = lax.dot_general(q, k, NT, preferred_element_type=jnp.float32)
        return s + own2d[t * TQ : (t + 1) * TQ, 0 : (t + 1) * TQ]

    def own_finish(h, t, s):
        rows = slice(t * TQ, (t + 1) * TQ)
        m = jnp.max(s, axis=1, keepdims=True)
        p = jnp.exp2((s - m) * SCALE2)
        v = kv_v[1, 0 : (t + 1) * TQ, columns(h)]
        l1[h, rows, :] = jnp.broadcast_to(jnp.sum(p, axis=1, keepdims=True), (TQ, HSZ))
        m1[h, rows, :] = jnp.broadcast_to(m, (TQ, HSZ))
        acc1[h, rows, :] = jnp.dot(p.astype(jnp.bfloat16), v, preferred_element_type=jnp.float32)

    @pl.loop(0, HEADS // 2)
    def _(t):
        pipelined([(2 * t + i, tile) for i in range(2) for tile in range(BLK // TQ)], own_scores, own_finish)

    def bq_copy(pb, d):
        ref = qbuf.at[ca, pb]
        return remote(ref, ref, bq_send, bq_recv, bdev(d))

    def aq_copy(pa, pb, d):
        ref = qbuf.at[pa, pb]
        return remote(ref, ref, aq_send, aq_recv.at[d - 1, pb], adev(d))

    received(qbuf.at[0, 0, :, pl.ds(0, (NZ - 1) * SHARE), :], zq_recv)
    for d in (2, 1, 3):
        bq_copy(cb, d).start()
    for d in (2, 1, 3):
        aq_copy(ca, cb, d).start()
    anchor_first(0)
    anchor_first(1)

    sk_copy.wait_recv()
    loads[2].wait()
    lane = lax.broadcasted_iota(jnp.int32, (QB, HSZ), 1)
    pair_lane = lax.broadcasted_iota(jnp.int32, (2 * QB, HSZ), 1)
    pair_row = lax.broadcasted_iota(jnp.int32, (2 * QB, HSZ), 0)

    def encode(o):
        a = jnp.maximum(jnp.max(jnp.abs(o), axis=-1, keepdims=True), 1e-30)
        return a, jnp.round(o * (CODE / a)).astype(jnp.int32).astype(jnp.int16)

    def suffix_pair(blocks, with_suffix):
        bx = jnp.where(first, *blocks[0])
        bys = [jnp.where(first, ib, ia) for ia, ib in blocks]

        def scores(e):
            q = jnp.concatenate([qbuf[ia, ib, e] for ia, ib in blocks], axis=0)
            parts = []
            for i, ref in enumerate((kv_v, kvs)):
                s = lax.dot_general(q, ref[0, :, columns(GH * bx + e)], NT, preferred_element_type=jnp.float32)
                parts.append(s + bias[:, i * BLK : (i + 1) * BLK])
            if with_suffix:
                by = jnp.where(pair_row < QB, bys[0], bys[1] - 1)
                qpos = by * (2 * QB) + lax.div(pair_row, SHARE) * (2 * SHARE) + c * SHARE + rem(pair_row, SHARE)
                other = (hst + 1 - 2 * c) * SHARE + pair_lane - SHARE
                kpos = jnp.where(pair_lane < SHARE, hst * SHARE + pair_lane, other)
                s = lax.dot_general(q, ksuf[0, :, e * HSZ : (e + 1) * HSZ], NT, preferred_element_type=jnp.float32)
                parts.append(jnp.where((pair_lane < 2 * SHARE) & (kpos <= qpos), s, NEG))
            return jnp.concatenate(parts, axis=1)

        columns_of = []

        def finish(e, s):
            m = jnp.maximum(jnp.max(s, axis=1, keepdims=True), FLOOR)
            p = jnp.exp2((s - m) * SCALE2)
            l = jnp.maximum(jnp.sum(p, axis=1, keepdims=True), 1.0)
            w = p.astype(jnp.bfloat16)
            h = GH * bx + e
            o = jnp.dot(w[:, :BLK], kv_v[1, :, columns(h)], preferred_element_type=jnp.float32)
            o = o + jnp.dot(w[:, BLK : 2 * BLK], kvs[1, :, columns(h)], preferred_element_type=jnp.float32)
            if with_suffix:
                v = ksuf[1, :, e * HSZ : (e + 1) * HSZ]
                o = o + jnp.dot(w[:, 2 * BLK :], v, preferred_element_type=jnp.float32)
            a, code = encode(o / l)
            lse = m * SCALE2 + jnp.log2(l)
            for i, (ia, ib) in enumerate(blocks):
                codes[ia, ib, e] = code[i * QB : (i + 1) * QB]
            columns_of.append((lse, a))

        pipelined([(e,) for e in range(GH)], scores, finish)
        for i, (ia, ib) in enumerate(blocks):
            rows = slice(i * QB, (i + 1) * QB)
            stats[ia, ib] = rows_of([(lse[rows], a[rows]) for lse, a in columns_of])

    def rows_of(columns_of):
        flat_stats = jnp.zeros((QB, HSZ), jnp.float32)
        for e, (lse, a) in enumerate(columns_of):
            flat_stats = jnp.where(lane == e, lse, jnp.where(lane == 4 + e, a, flat_stats))
        return flat_stats.T[0:8]

    def merge(parts):
        lses = [s[0:4] for s in parts]
        top = lses[0]
        for s in lses[1:]:
            top = jnp.maximum(top, s)
        weights = [jnp.exp2(s - top) for s in lses]
        total = weights[0]
        for w in weights[1:]:
            total = total + w
        inverse = 1.0 / (total * CODE)
        rows = jnp.concatenate([w * inverse * s[4:8] for w, s in zip(weights, parts)], axis=0)
        rows = jnp.concatenate([rows, jnp.zeros((HSZ - rows.shape[0], HSZ), jnp.float32)], axis=0)
        return rows.T, top + jnp.log2(total)

    def blend(coefficients, coded, e):
        total = None
        for i, code in enumerate(coded):
            term = coefficients[:, 4 * i + e : 4 * i + e + 1] * code.astype(jnp.int32).astype(jnp.float32)
            total = term if total is None else total + term
        return total

    def blend_and_encode(parts, coded_of, store):
        coefficients, lse = merge(parts)
        scales = []
        for e in range(GH):
            a, code = encode(blend(coefficients, coded_of(e), e))
            store(e, code)
            scales.append((a, a))
        return jnp.concatenate([lse, rows_of(scales)[0:4]], axis=0)

    def rb_copies(ia, d):
        ib = rem(cb + d, NX)
        return [
            remote(codes.at[ia, ib], rb.at[d - 1, ia], rb_send.at[0], rb_recv.at[0, ia], bdev(d)),
            remote(stats.at[ia, ib], rbs.at[d - 1, ia], rb_send.at[1], rb_recv.at[1, ia], bdev(d)),
        ]

    def ra_copies(d):
        ia = rem(ca + d, NX)
        return [
            remote(codes2.at[ia], ra.at[d - 1], ra_send.at[0], ra_recv.at[0], adev(d)),
            remote(stats2.at[ia], ras.at[d - 1], ra_send.at[1], ra_recv.at[1], adev(d)),
        ]

    def rz_copies(d):
        rows = pl.ds(pl.multiple_of(rem(z + d, NZ) * SHARE, SHARE), SHARE)
        return [
            remote(codes3.at[:, rows, :], rz.at[d - 1], rz_send.at[0], rz_recv.at[0], zdev(d)),
            remote(stats3, rzs.at[d - 1], rz_send.at[1], rz_recv.at[1], zdev(d)),
        ]

    def reduce_b(delta):
        ia = rem(ca + delta, NX)
        received(rb.at[:, ia], rb_recv.at[0, ia])
        received(rbs.at[:, ia], rb_recv.at[1, ia])

        def store(e, code):
            codes2[ia, e] = code

        stats2[ia] = blend_and_encode(
            [stats[ia, cb]] + [rbs[d, ia] for d in range(NX - 1)],
            lambda e: [codes[ia, cb, e]] + [rb[d, ia, e] for d in range(NX - 1)],
            store,
        )
        if delta:
            for copy in ra_copies(delta):
                copy.start()

    def reduce_a():
        received(ra, ra_recv.at[0])
        received(ras, ra_recv.at[1])

        def store(e, code):
            codes3[e] = code

        stats3[...] = blend_and_encode(
            [stats2[ca]] + [ras[d] for d in range(NX - 1)],
            lambda e: [codes2[ca, e]] + [ra[d, e] for d in range(NX - 1)],
            store,
        )
        for d in (4, 3, 5, 2, 6, 1, 7):
            for copy in rz_copies(d):
                copy.start()

    def reduce_z():
        received(rz, rz_recv.at[0])
        received(rzs, rz_recv.at[1])
        turned[...], unused = merge([stats3[...]] + [rzs[d] for d in range(NZ - 1)])
        rows = pl.ds(zrow, SHARE)
        coefficients = turned[rows, :]
        for e in range(GH):
            o = blend(coefficients, [codes3[e, rows, :]] + [rz[d, e] for d in range(NZ - 1)], e)
            suf_v[:, e * HSZ : (e + 1) * HSZ] = o.astype(suf_v.dtype)
        pltpu.make_async_copy(suf_v, suf_out, suf_sem).start()

    def q_b():
        received(qbuf.at[0, pl.ds(0, NX - 1)], bq_recv)
        for i in range(1, NX):
            for d in (2, 1, 3):
                aq_copy(ca, rem(cb + i, NX), d).start()

    def all_of(*steps):
        def run():
            for step, *arguments in steps:
                step(*arguments)

        return run

    q_b()
    kvs_copy.wait_recv()
    anchor_first(2)
    anchor_second(0)

    before = {
        0: all_of((anchor_second, 1)),
        1: all_of((anchor_second, 2)),
        3: all_of((anchor_z, 0)),
        4: all_of((anchor_z, 1)),
        5: all_of((anchor_z, 2), (anchor_b, 0)),
        6: all_of((anchor_b, 1)),
        7: all_of((anchor_b, 2), (reduce_b, 1)),
    }

    @pl.loop(0, NX * NY // 2)
    def _(n):
        for at, event in before.items():
            pl.when(n == at)(event)
        group, shift = lax.div(n, 2), jnp.where(n < 4, 0, 1)
        delta, late = jnp.where(group < 2, group, 5 - group), 3 * shift
        deltas = (jnp.where(first, delta, late), jnp.where(first, delta, 1 + shift))
        step, place_b = 2 * rem(n, 2) + shift, rem(n + shift, 4)
        steps = (jnp.where(first, step, place_b), jnp.where(first, rem(step + 1, 4), place_b))
        blocks = [(rem(ca + delta, NX), rem(cb + step, NX)) for delta, step in zip(deltas, steps)]
        for delta, (ia, ib) in zip(deltas, blocks):

            @pl.when(delta > 0)
            def _():
                aq_copy(ia, ib, jnp.where(delta > 0, NX - delta, 1)).wait_recv()

        own_heads = jnp.where(first, *blocks[0]) == x

        @pl.when(own_heads)
        def _():
            suffix_pair(blocks, True)

        @pl.when(jnp.logical_not(own_heads))
        def _():
            suffix_pair(blocks, False)

        for step, (ia, ib) in zip(steps, blocks):

            @pl.when(step > 0)
            def _():
                for copy in rb_copies(ia, jnp.where(step > 0, step, 1)):
                    copy.start()

    anchor_a(0)
    reduce_b(0)
    reduce_b(3)

    def anchor_scores(h, t):
        q = q_v[t * TQ : (t + 1) * TQ, columns(h)]
        return lax.dot_general(q, anc[0, :, columns(h)], NT, preferred_element_type=jnp.float32) + abias[...]

    def anchor_finish(h, t, s):
        rows = slice(t * TQ, (t + 1) * TQ)
        before = m1[h, rows, :]
        m = jnp.maximum(before, jnp.max(s, axis=1, keepdims=True))
        p = jnp.exp2((s - wide(m, BLK // HSZ)) * SCALE2)
        fade = jnp.exp2((before - m) * SCALE2)
        l = l1[h, rows, :] * fade + jnp.sum(p, axis=1, keepdims=True)
        o = jnp.dot(p.astype(jnp.bfloat16), anc[1, :, columns(h)], preferred_element_type=jnp.float32)
        o = (acc1[h, rows, :] * fade + o) / l
        token = lax.broadcasted_iota(jnp.int32, (TQ, HSZ), 0) + t * TQ
        obuf[h, rows, :] = jnp.where(token < own_len, o, 0.0).astype(obuf.dtype)

    def out_copy(h):
        return pltpu.make_async_copy(obuf.at[h], ctx_out.at[:, columns(h)], out_sem)

    tail = {
        1: all_of((anchor_a, 1), (reduce_b, 2)),
        2: all_of((anchor_a, 2)),
        4: all_of((reduce_a,)),
    }

    @pl.loop(0, HEADS // 2)
    def _(t):
        for at, event in tail.items():
            pl.when(t == at)(event)
        k, other = lax.div(t, 2), rem(t, 2)

        @pl.when(other == 1)
        def _():
            sib_copy(k, 1 - c).wait_recv()

        h = rem(c + other, 2) * (HEADS // 2) + 2 * k
        pipelined([(h + i, tile) for i in range(2) for tile in range(BLK // TQ)], anchor_scores, anchor_finish)
        for i in range(2):
            out_copy(h + i).start()

    reduce_z()

    for copy in (kvs_copy, sk_copy):
        copy.wait_send()
    sent(qbuf.at[0, 0, :, pl.ds(0, (NZ - 1) * SHARE), :], zq_send)
    sent(qbuf.at[0, pl.ds(0, NX - 1)], bq_send)
    sent(qbuf.at[pl.ds(0, NX - 1)], aq_send)
    sent(codes.at[pl.ds(0, NX - 1)], rb_send.at[0])
    sent(stats.at[pl.ds(0, NX - 1)], rb_send.at[1])
    sent(ra, ra_send.at[0])
    sent(ras, ra_send.at[1])
    sent(rz, rz_send.at[0])
    sent(rzs, rz_send.at[1])
    half = pl.ds(0, HD // 2)
    sent(anc.at[:, pl.ds(0, (NX - 1) * PROWS), half], bb_send)
    sent(anc.at[:, pl.ds(0, (NX - 1) * AROWS), half], ab_send)
    sent(anc.at[:, :, half], sib_send)

    @pl.when(z == 0)
    def _():
        sent(anc.at[:, pl.ds(0, (NZ - 1) * PROWS // 2), :], zb_send)

        @pl.when(cb == 0)
        def _():
            sent(anc.at[:, pl.ds(0, (NX - 1) * PROWS), half], sb_send)

    @pl.when(is_root)
    def _():
        sent(kv_v.at[:, pl.ds(0, (2 * NX - 1) * AROWS // 2), :], sc_send)

    pltpu.make_async_copy(suf_v, suf_out, suf_sem).wait()
    pltpu.make_async_copy(q_v, ctx_out, out_sem).wait()


def per_device(queries, keys_values, token_ids, lengths, suffix_queries, suffix_kv):
    bf16, f32, i16 = jnp.bfloat16, jnp.float32, jnp.int16
    dma = pltpu.SemaphoreType.DMA
    scratch = [
        pltpu.VMEM((BLK, HD), bf16),
        pltpu.VMEM((2, BLK, HD), bf16),
        pltpu.VMEM((2, BLK, HD), bf16),
        pltpu.VMEM((24, HSZ), jnp.int32),
        pltpu.VMEM((2, HSZ, GH * HSZ), bf16),
        pltpu.VMEM((NX, NX, GH, QB, HSZ), bf16),
        pltpu.VMEM((2, BLK, HD), bf16),
        pltpu.VMEM((NCH, 2, AROWS, CW), bf16),
        pltpu.VMEM((HEADS, BLK, HSZ), f32),
        pltpu.VMEM((HEADS, BLK, HSZ), f32),
        pltpu.VMEM((HEADS, BLK, HSZ), f32),
        pltpu.VMEM((BLK, BLK), f32),
        pltpu.VMEM((1, 2 * BLK), f32),
        pltpu.VMEM((1, BLK), f32),
        pltpu.VMEM((NX, NX, GH, QB, HSZ), i16),
        pltpu.VMEM((NX, NX, 8, HSZ), f32),
        pltpu.VMEM((NX - 1, NX, GH, QB, HSZ), i16),
        pltpu.VMEM((NX - 1, NX, 8, HSZ), f32),
        pltpu.VMEM((NX, GH, QB, HSZ), i16),
        pltpu.VMEM((NX, 8, HSZ), f32),
        pltpu.VMEM((NX - 1, GH, QB, HSZ), i16),
        pltpu.VMEM((NX - 1, 8, HSZ), f32),
        pltpu.VMEM((GH, QB, HSZ), i16),
        pltpu.VMEM((8, HSZ), f32),
        pltpu.VMEM((NZ - 1, GH, SHARE, HSZ), i16),
        pltpu.VMEM((NZ - 1, 8, HSZ), f32),
        pltpu.VMEM((HSZ, HSZ), f32),
        pltpu.VMEM((HEADS, BLK, HSZ), bf16),
        pltpu.VMEM((SHARE, GH * HSZ), bf16),
        dma((5,)),
        dma, dma, dma, dma,
        dma, dma,
        dma, dma,
        dma, dma((NX - 1, NX)),
        dma, dma((NCH,)), dma((NCH,)),
        dma, dma((NCH,)),
        dma, dma((NCH,)),
        dma, dma((NCH,)),
        dma, dma((NCH,)),
        dma, dma((NCH,)),
        dma((2,)), dma((2, NX)),
        dma((2,)), dma((2,)),
        dma((2,)), dma((2,)),
        dma, dma,
    ]
    anywhere = pl.BlockSpec(memory_space=pl.ANY)
    return pl.pallas_call(
        kernel,
        out_shape=(
            pltpu.VMEM((BLK, HD), bf16),
            pltpu.VMEM((SHARE, GH * HSZ), bf16),
        ),
        in_specs=[anywhere, anywhere, anywhere, pl.BlockSpec(memory_space=pltpu.SMEM), anywhere, anywhere],
        out_specs=(anywhere, anywhere),
        scratch_shapes=scratch,
        compiler_params=pltpu.CompilerParams(
            collective_id=0, has_side_effects=True, vmem_limit_bytes=56 * 2**20
        ),
        cost_estimate=pl.CostEstimate(
            flops=6_500_000_000, bytes_accessed=6_500_000, transcendentals=12_600_000
        ),
        name="star",
    )(queries, keys_values, token_ids.reshape(-1, HSZ), lengths, suffix_queries, suffix_kv)


def solution(mesh):
    return jax.shard_map(
        per_device,
        mesh=mesh,
        in_specs=(
            P(("hst", "grp"), None),
            P(None, ("hst", "grp"), None),
            P(),
            P(),
            P("hst", "grp"),
            P(None, "hst", "grp"),
        ),
        out_specs=(P(("hst", "grp"), None), P("hst", "grp")),
        check_vma=False,
    )
```

```python
import math

import jax
import jax.numpy as jnp
from jax import lax
from jax.experimental import pallas as pl
from jax.experimental.pallas import tpu as pltpu
from jax.sharding import PartitionSpec as P

HEADS = 12
HSZ = 128
BLK = 512
HD = HEADS * HSZ
NAMB = 512
NEG = -1e30
FLOOR = -1e29
SCALE2 = math.log2(math.e) / math.sqrt(HSZ)
CODE = 32767.0
SIZES = (4, 4, 8)
NX, NY, NZ = SIZES
GH = HEADS // NX
SHARE = 16
QB = NZ * SHARE
TQ = 256
EARLY = 2
NCH = 3
CW = HD // 2 // NCH
PROWS = BLK // (NX * NY)
AROWS = BLK // NX
NT = (((1,), (1,)), ((), ()))
MESH = pl.DeviceIdType.MESH


def rem(a, n):
    return lax.rem(a, jnp.int32(n))


def kernel(
    q_hbm, kv_hbm, tok_hbm, lens, sq_hbm, skv_hbm,
    ctx_out, suf_out,
    q_v, kv_v, kvs, tok_v, ksuf, qbuf, anc, stage, acc1, m1, l1, own2d, bias, abias,
    codes, stats, rb, rbs, codes2, stats2, ra, ras, codes3, stats3, rz, rzs, turned, obuf, suf_v,
    in_sem, kvs_send, kvs_recv, sk_send, sk_recv,
    zq_send, zq_recv, bq_send, bq_recv, aq_send, aq_recv,
    sc_send, sc_recv, own_sem, sb_send, sb_recv, zb_send, zb_recv, bb_send, bb_recv, ab_send, ab_recv, sib_send, sib_recv,
    rb_send, rb_recv, ra_send, ra_recv, rz_send, rz_recv,
    out_sem, suf_sem,
):
    hst = lax.axis_index("hst")
    x = lax.axis_index("grp")
    c = rem(hst, 2)
    z = rem(lax.div(hst, 2), NZ)
    y = lax.div(hst, 2 * NZ)
    block = hst * NX + x
    first = c == 0
    ca = jnp.where(first, x, y)
    cb = jnp.where(first, y, x)

    def dev(px, py, pz, pc):
        return ((py * NZ + pz) * 2 + pc, px)

    def place(pa, pb, pz, pc):
        on = pc == 0
        return dev(jnp.where(on, pa, pb), jnp.where(on, pb, pa), pz, pc)

    def adev(delta):
        return place(rem(ca + delta, NX), cb, z, c)

    def bdev(delta):
        return place(ca, rem(cb + delta, NX), z, c)

    def zdev(delta):
        return dev(x, y, rem(z + delta, NZ), c)

    sibling = dev(x, y, z, 1 - c)

    def remote(src, dst, send, recv, to):
        return pltpu.make_async_remote_copy(
            src_ref=src, dst_ref=dst, send_sem=send, recv_sem=recv, device_id=to, device_id_type=MESH
        )

    def sent(ref, send):
        remote(ref, ref, send, kvs_recv, sibling).wait_send()

    def received(ref, recv):
        remote(ref, ref, kvs_send, recv, sibling).wait_recv()

    sblock = (hst + 1 - 2 * c) * NX + x
    zrow = pl.multiple_of(z * SHARE, SHARE)
    qloads = [
        pltpu.make_async_copy(
            sq_hbm.at[:, pl.ds(e * HSZ, HSZ)], qbuf.at[ca, cb, e, pl.ds(zrow, SHARE), :], in_sem.at[4]
        )
        for e in range(GH)
    ]
    loads = [
        pltpu.make_async_copy(q_hbm, q_v, in_sem.at[0]),
        pltpu.make_async_copy(kv_hbm, kv_v, in_sem.at[1]),
        pltpu.make_async_copy(skv_hbm, ksuf.at[:, pl.ds(0, SHARE), :], in_sem.at[2]),
    ]
    for i, b in enumerate((block, sblock, 0)):
        row = pl.multiple_of(lax.div(b, 2) * 8, 8)
        loads.append(pltpu.make_async_copy(tok_hbm.at[pl.ds(row, 8), :], tok_v.at[pl.ds(8 * i, 8), :], in_sem.at[3]))
    barrier = pltpu.get_barrier_semaphore()
    far_first = (4, 3, 5, 2, 6, 1, 7)
    partners = [zdev(d) for d in far_first]
    partners += [dev_of(d) for d in (2, 1, 3) for dev_of in (adev, bdev)] + [sibling]
    for partner in partners:
        pl.semaphore_signal(barrier, inc=1, device_id=partner, device_id_type=MESH)
    is_root = block == 0
    is_extra = (z == 0) & (x == 0) & (y > 0) & (c == 1)

    @pl.when(is_extra)
    def _():
        pl.semaphore_signal(barrier, inc=1, device_id=(0, 0), device_id_type=MESH)

    for copy in qloads + loads:
        copy.start()

    pltpu.make_async_copy(tok_hbm.at[pl.ds(0, 24), :], tok_v, in_sem.at[3]).wait()
    flat = lax.broadcasted_iota(jnp.int32, (4, HSZ), 0) * HSZ + lax.broadcasted_iota(jnp.int32, (4, HSZ), 1)

    def key_bias(i, b, length, on):
        both = tok_v[8 * i : 8 * i + 8]
        ids = jnp.where(rem(b, 2) == 1, both[4:8], both[0:4])
        part = jnp.where((ids >= NAMB) & (flat < length) & on, 0.0, NEG)
        return jnp.concatenate([part[r : r + 1] for r in range(4)], axis=1)

    own_len = lens[block]
    own_bias = key_bias(0, block, own_len, True)
    bias[:, 0:BLK] = own_bias
    bias[:, BLK:] = key_bias(1, sblock, lens[sblock], True)
    abias[...] = key_bias(2, jnp.int32(0), lens[0], block > 0)
    row2d = lax.broadcasted_iota(jnp.int32, (BLK, BLK), 0)
    col2d = lax.broadcasted_iota(jnp.int32, (BLK, BLK), 1)
    own2d[...] = jnp.where(col2d == row2d, 0.0, jnp.where(col2d < row2d, own_bias, NEG))
    ksuf[:, 2 * SHARE :, :] = jnp.zeros((2, HSZ - 2 * SHARE, GH * HSZ), ksuf.dtype)

    def columns(h):
        return pl.ds(pl.multiple_of(h * HSZ, HSZ), HSZ)

    def wide(a, copies):
        return jnp.concatenate([a] * copies, axis=1)

    def pipelined(units, scores, finish):
        ready = scores(*units[0])
        for i, unit in enumerate(units):
            later = scores(*units[i + 1]) if i + 1 < len(units) else None
            finish(*unit, ready)
            ready = later

    loads[0].wait()
    loads[1].wait()

    def own_scores(h, t):
        q = q_v[t * TQ : (t + 1) * TQ, columns(h)]
        k = kv_v[0, 0 : (t + 1) * TQ, columns(h)]
        s = lax.dot_general(q, k, NT, preferred_element_type=jnp.float32)
        return s + own2d[t * TQ : (t + 1) * TQ, 0 : (t + 1) * TQ]

    def own_finish(h, t, s):
        rows = slice(t * TQ, (t + 1) * TQ)
        m = jnp.max(s, axis=1, keepdims=True)
        p = jnp.exp2((s - m) * SCALE2)
        v = kv_v[1, 0 : (t + 1) * TQ, columns(h)]
        l1[h, rows, :] = jnp.broadcast_to(jnp.sum(p, axis=1, keepdims=True), (TQ, HSZ))
        m1[h, rows, :] = jnp.broadcast_to(m, (TQ, HSZ))
        acc1[h, rows, :] = jnp.dot(p.astype(jnp.bfloat16), v, preferred_element_type=jnp.float32)

    @pl.loop(0, EARLY)
    def _(t):
        pipelined([(2 * t + i, tile) for i in range(2) for tile in range(BLK // TQ)], own_scores, own_finish)

    pl.semaphore_wait(barrier, len(partners) + jnp.where(is_root, NY - 1, 0))

    ref = qbuf.at[ca, cb, :, pl.ds(zrow, SHARE), :]
    pltpu.make_async_copy(ref, ref, in_sem.at[4]).wait()
    zq = []
    for d in far_first:
        ref = qbuf.at[ca, cb, :, pl.ds(zrow, SHARE), :]
        zq.append(remote(ref, ref, zq_send, zq_recv, zdev(d)))
        zq[-1].start()

    kvs_copy = remote(kv_hbm, kvs, kvs_send, kvs_recv, sibling)
    kvs_copy.start()
    sk_copy = remote(skv_hbm, ksuf.at[:, pl.ds(SHARE, SHARE), :], sk_send, sk_recv, sibling)
    sk_copy.start()

    def piece(ref, k, pa, pb, core, rows):
        row = pl.multiple_of(pa * AROWS + pb * PROWS, PROWS)
        col = pl.multiple_of(core * (HD // 2) + k * CW, HSZ)
        return ref.at[:, pl.ds(row, rows), pl.ds(col, CW)]

    def scatter_copy(k, i):
        core, pa = rem(i, 2), lax.div(i, 2)
        src = piece(kv_hbm, k, pa, 0, core, AROWS)
        return remote(src, stage.at[k], sc_send, sc_recv.at[k], place(pa, 0, 0, core))

    def root_own(k):
        return pltpu.make_async_copy(piece(kv_hbm, k, 0, 0, 0, AROWS), stage.at[k], own_sem.at[k])

    @pl.when(is_root)
    def _():
        for k in range(NCH):
            root_own(k).start()
            for i in (4, 5, 2, 3, 6, 7, 1):
                scatter_copy(k, jnp.int32(i)).start()

    def sb_copy(k, d):
        src = stage.at[k, :, pl.ds(d * PROWS, PROWS), :]
        return remote(src, piece(anc, k, ca, rem(cb + d, NX), c, PROWS), sb_send, sb_recv.at[k], bdev(d))

    def zb_copy(k, d):
        ref = piece(anc, k, ca, cb, c, PROWS)
        return remote(ref, ref, zb_send, zb_recv.at[k], zdev(d))

    def bb_copy(k, pb, d):
        ref = piece(anc, k, ca, pb, c, PROWS)
        return remote(ref, ref, bb_send, bb_recv.at[k], bdev(d))

    def ab_copy(k, pa, d):
        ref = piece(anc, k, pa, 0, c, AROWS)
        return remote(ref, ref, ab_send, ab_recv.at[k], adev(d))

    def sib_copy(k, core):
        ref = piece(anc, k, 0, 0, core, BLK)
        return remote(ref, ref, sib_send, sib_recv.at[k], sibling)

    def anchor_first(k):
        @pl.when((z == 0) & (cb == 0))
        def _():
            @pl.when(is_root)
            def _():
                root_own(k).wait()

            @pl.when(jnp.logical_not(is_root))
            def _():
                remote(stage.at[k], stage.at[k], sib_send, sc_recv.at[k], sibling).wait_recv()

            for d in (2, 1, 3):
                sb_copy(k, d).start()
            row = pl.multiple_of(ca * AROWS, AROWS)
            col = pl.multiple_of(c * (HD // 2) + k * CW, HSZ)
            anc[:, pl.ds(row, PROWS), pl.ds(col, CW)] = stage[k, :, 0:PROWS, :]

    def anchor_second(k):
        @pl.when(z == 0)
        def _():
            @pl.when(cb > 0)
            def _():
                ref = piece(anc, k, ca, cb, c, PROWS)
                remote(ref, ref, sib_send, sb_recv.at[k], sibling).wait_recv()

            for d in (4, 3, 5, 2, 6, 1, 7):
                zb_copy(k, d).start()

    def anchor_z(k):
        @pl.when(z > 0)
        def _():
            zb_copy(k, 1).wait_recv()

        for d in (2, 1, 3):
            bb_copy(k, cb, d).start()

    def anchor_b(k):
        received(anc.at[:, pl.ds(0, (NX - 1) * PROWS), pl.ds(0, CW)], bb_recv.at[k])
        for d in (2, 1, 3):
            ab_copy(k, ca, d).start()

    def anchor_a(k):
        received(anc.at[:, pl.ds(0, (NX - 1) * AROWS), pl.ds(0, CW)], ab_recv.at[k])
        sib_copy(k, c).start()

    @pl.loop(EARLY, HEADS // 2)
    def _(t):
        pipelined([(2 * t + i, tile) for i in range(2) for tile in range(BLK // TQ)], own_scores, own_finish)

    def bq_copy(pb, d):
        ref = qbuf.at[ca, pb]
        return remote(ref, ref, bq_send, bq_recv, bdev(d))

    def aq_copy(pa, pb, d):
        ref = qbuf.at[pa, pb]
        return remote(ref, ref, aq_send, aq_recv.at[d - 1, pb], adev(d))

    received(qbuf.at[0, 0, :, pl.ds(0, (NZ - 1) * SHARE), :], zq_recv)
    for d in (2, 1, 3):
        bq_copy(cb, d).start()
    for d in (2, 1, 3):
        aq_copy(ca, cb, d).start()
    anchor_first(0)
    anchor_first(1)

    sk_copy.wait_recv()
    loads[2].wait()
    lane = lax.broadcasted_iota(jnp.int32, (QB, HSZ), 1)
    pair_lane = lax.broadcasted_iota(jnp.int32, (2 * QB, HSZ), 1)
    pair_row = lax.broadcasted_iota(jnp.int32, (2 * QB, HSZ), 0)

    def encode(o):
        a = jnp.maximum(jnp.max(jnp.abs(o), axis=-1, keepdims=True), 1e-30)
        return a, jnp.round(o * (CODE / a)).astype(jnp.int32).astype(jnp.int16)

    def suffix_pair(blocks, with_suffix):
        bx = jnp.where(first, *blocks[0])
        bys = [jnp.where(first, ib, ia) for ia, ib in blocks]

        def scores(e):
            q = jnp.concatenate([qbuf[ia, ib, e] for ia, ib in blocks], axis=0)
            parts = []
            for i, ref in enumerate((kv_v, kvs)):
                s = lax.dot_general(q, ref[0, :, columns(GH * bx + e)], NT, preferred_element_type=jnp.float32)
                parts.append(s + bias[:, i * BLK : (i + 1) * BLK])
            if with_suffix:
                by = jnp.where(pair_row < QB, bys[0], bys[1] - 1)
                qpos = by * (2 * QB) + lax.div(pair_row, SHARE) * (2 * SHARE) + c * SHARE + rem(pair_row, SHARE)
                other = (hst + 1 - 2 * c) * SHARE + pair_lane - SHARE
                kpos = jnp.where(pair_lane < SHARE, hst * SHARE + pair_lane, other)
                s = lax.dot_general(q, ksuf[0, :, e * HSZ : (e + 1) * HSZ], NT, preferred_element_type=jnp.float32)
                parts.append(jnp.where((pair_lane < 2 * SHARE) & (kpos <= qpos), s, NEG))
            return jnp.concatenate(parts, axis=1)

        columns_of = []

        def finish(e, s):
            m = jnp.maximum(jnp.max(s, axis=1, keepdims=True), FLOOR)
            p = jnp.exp2((s - m) * SCALE2)
            l = jnp.maximum(jnp.sum(p, axis=1, keepdims=True), 1.0)
            w = p.astype(jnp.bfloat16)
            h = GH * bx + e
            o = jnp.dot(w[:, :BLK], kv_v[1, :, columns(h)], preferred_element_type=jnp.float32)
            o = o + jnp.dot(w[:, BLK : 2 * BLK], kvs[1, :, columns(h)], preferred_element_type=jnp.float32)
            if with_suffix:
                v = ksuf[1, :, e * HSZ : (e + 1) * HSZ]
                o = o + jnp.dot(w[:, 2 * BLK :], v, preferred_element_type=jnp.float32)
            a, code = encode(o / l)
            lse = m * SCALE2 + jnp.log2(l)
            for i, (ia, ib) in enumerate(blocks):
                codes[ia, ib, e] = code[i * QB : (i + 1) * QB]
            columns_of.append((lse, a))

        pipelined([(e,) for e in range(GH)], scores, finish)
        for i, (ia, ib) in enumerate(blocks):
            rows = slice(i * QB, (i + 1) * QB)
            stats[ia, ib] = rows_of([(lse[rows], a[rows]) for lse, a in columns_of])

    def rows_of(columns_of):
        flat_stats = jnp.zeros((QB, HSZ), jnp.float32)
        for e, (lse, a) in enumerate(columns_of):
            flat_stats = jnp.where(lane == e, lse, jnp.where(lane == 4 + e, a, flat_stats))
        return flat_stats.T[0:8]

    def merge(parts):
        lses = [s[0:4] for s in parts]
        top = lses[0]
        for s in lses[1:]:
            top = jnp.maximum(top, s)
        weights = [jnp.exp2(s - top) for s in lses]
        total = weights[0]
        for w in weights[1:]:
            total = total + w
        inverse = 1.0 / (total * CODE)
        rows = jnp.concatenate([w * inverse * s[4:8] for w, s in zip(weights, parts)], axis=0)
        rows = jnp.concatenate([rows, jnp.zeros((HSZ - rows.shape[0], HSZ), jnp.float32)], axis=0)
        return rows.T, top + jnp.log2(total)

    def blend(coefficients, coded, e):
        total = None
        for i, code in enumerate(coded):
            term = coefficients[:, 4 * i + e : 4 * i + e + 1] * code.astype(jnp.int32).astype(jnp.float32)
            total = term if total is None else total + term
        return total

    def blend_and_encode(parts, coded_of, store):
        coefficients, lse = merge(parts)
        scales = []
        for e in range(GH):
            a, code = encode(blend(coefficients, coded_of(e), e))
            store(e, code)
            scales.append((a, a))
        return jnp.concatenate([lse, rows_of(scales)[0:4]], axis=0)

    def rb_copies(ia, d):
        ib = rem(cb + d, NX)
        return [
            remote(codes.at[ia, ib], rb.at[d - 1, ia], rb_send.at[0], rb_recv.at[0, ia], bdev(d)),
            remote(stats.at[ia, ib], rbs.at[d - 1, ia], rb_send.at[1], rb_recv.at[1, ia], bdev(d)),
        ]

    def ra_copies(d):
        ia = rem(ca + d, NX)
        return [
            remote(codes2.at[ia], ra.at[d - 1], ra_send.at[0], ra_recv.at[0], adev(d)),
            remote(stats2.at[ia], ras.at[d - 1], ra_send.at[1], ra_recv.at[1], adev(d)),
        ]

    def rz_copies(d):
        rows = pl.ds(pl.multiple_of(rem(z + d, NZ) * SHARE, SHARE), SHARE)
        return [
            remote(codes3.at[:, rows, :], rz.at[d - 1], rz_send.at[0], rz_recv.at[0], zdev(d)),
            remote(stats3, rzs.at[d - 1], rz_send.at[1], rz_recv.at[1], zdev(d)),
        ]

    def reduce_b(delta):
        ia = rem(ca + delta, NX)
        received(rb.at[:, ia], rb_recv.at[0, ia])
        received(rbs.at[:, ia], rb_recv.at[1, ia])

        def store(e, code):
            codes2[ia, e] = code

        stats2[ia] = blend_and_encode(
            [stats[ia, cb]] + [rbs[d, ia] for d in range(NX - 1)],
            lambda e: [codes[ia, cb, e]] + [rb[d, ia, e] for d in range(NX - 1)],
            store,
        )
        if delta:
            for copy in ra_copies(delta):
                copy.start()

    def reduce_a():
        received(ra, ra_recv.at[0])
        received(ras, ra_recv.at[1])

        def store(e, code):
            codes3[e] = code

        stats3[...] = blend_and_encode(
            [stats2[ca]] + [ras[d] for d in range(NX - 1)],
            lambda e: [codes2[ca, e]] + [ra[d, e] for d in range(NX - 1)],
            store,
        )
        for d in (4, 3, 5, 2, 6, 1, 7):
            for copy in rz_copies(d):
                copy.start()

    def reduce_z():
        received(rz, rz_recv.at[0])
        received(rzs, rz_recv.at[1])
        turned[...], unused = merge([stats3[...]] + [rzs[d] for d in range(NZ - 1)])
        rows = pl.ds(zrow, SHARE)
        coefficients = turned[rows, :]
        for e in range(GH):
            o = blend(coefficients, [codes3[e, rows, :]] + [rz[d, e] for d in range(NZ - 1)], e)
            suf_v[:, e * HSZ : (e + 1) * HSZ] = o.astype(suf_v.dtype)
        pltpu.make_async_copy(suf_v, suf_out, suf_sem).start()

    def q_b():
        received(qbuf.at[0, pl.ds(0, NX - 1)], bq_recv)
        for i in range(1, NX):
            for d in (2, 1, 3):
                aq_copy(ca, rem(cb + i, NX), d).start()

    def all_of(*steps):
        def run():
            for step, *arguments in steps:
                step(*arguments)

        return run

    q_b()
    kvs_copy.wait_recv()
    anchor_first(2)
    anchor_second(0)

    before = {
        0: all_of((anchor_second, 1)),
        1: all_of((anchor_second, 2)),
        3: all_of((anchor_z, 0)),
        4: all_of((anchor_z, 1)),
        5: all_of((anchor_z, 2), (anchor_b, 0)),
        6: all_of((anchor_b, 1)),
        7: all_of((anchor_b, 2), (reduce_b, 1)),
    }

    @pl.loop(0, NX * NY // 2)
    def _(n):
        for at, event in before.items():
            pl.when(n == at)(event)
        group, shift = lax.div(n, 2), jnp.where(n < 4, 0, 1)
        delta, late = jnp.where(group < 2, group, 5 - group), 3 * shift
        deltas = (jnp.where(first, delta, late), jnp.where(first, delta, 1 + shift))
        step, place_b = 2 * rem(n, 2) + shift, rem(n + shift, 4)
        steps = (jnp.where(first, step, place_b), jnp.where(first, rem(step + 1, 4), place_b))
        blocks = [(rem(ca + delta, NX), rem(cb + step, NX)) for delta, step in zip(deltas, steps)]
        for delta, (ia, ib) in zip(deltas, blocks):

            @pl.when(delta > 0)
            def _():
                aq_copy(ia, ib, jnp.where(delta > 0, NX - delta, 1)).wait_recv()

        own_heads = jnp.where(first, *blocks[0]) == x

        @pl.when(own_heads)
        def _():
            suffix_pair(blocks, True)

        @pl.when(jnp.logical_not(own_heads))
        def _():
            suffix_pair(blocks, False)

        for step, (ia, ib) in zip(steps, blocks):

            @pl.when(step > 0)
            def _():
                for copy in rb_copies(ia, jnp.where(step > 0, step, 1)):
                    copy.start()

    anchor_a(0)
    reduce_b(0)
    reduce_b(3)

    def anchor_scores(h, t):
        q = q_v[t * TQ : (t + 1) * TQ, columns(h)]
        return lax.dot_general(q, anc[0, :, columns(h)], NT, preferred_element_type=jnp.float32) + abias[...]

    def anchor_finish(h, t, s):
        rows = slice(t * TQ, (t + 1) * TQ)
        before = m1[h, rows, :]
        m = jnp.maximum(before, jnp.max(s, axis=1, keepdims=True))
        p = jnp.exp2((s - wide(m, BLK // HSZ)) * SCALE2)
        fade = jnp.exp2((before - m) * SCALE2)
        l = l1[h, rows, :] * fade + jnp.sum(p, axis=1, keepdims=True)
        o = jnp.dot(p.astype(jnp.bfloat16), anc[1, :, columns(h)], preferred_element_type=jnp.float32)
        o = (acc1[h, rows, :] * fade + o) / l
        token = lax.broadcasted_iota(jnp.int32, (TQ, HSZ), 0) + t * TQ
        obuf[h, rows, :] = jnp.where(token < own_len, o, 0.0).astype(obuf.dtype)

    def out_copy(h):
        return pltpu.make_async_copy(obuf.at[h], ctx_out.at[:, columns(h)], out_sem)

    tail = {
        1: all_of((anchor_a, 1), (reduce_b, 2)),
        2: all_of((anchor_a, 2)),
        4: all_of((reduce_a,)),
    }

    @pl.loop(0, HEADS // 2)
    def _(t):
        for at, event in tail.items():
            pl.when(t == at)(event)
        k, other = lax.div(t, 2), rem(t, 2)

        @pl.when(other == 1)
        def _():
            sib_copy(k, 1 - c).wait_recv()

        h = rem(c + other, 2) * (HEADS // 2) + 2 * k
        pipelined([(h + i, tile) for i in range(2) for tile in range(BLK // TQ)], anchor_scores, anchor_finish)
        for i in range(2):
            out_copy(h + i).start()

    reduce_z()

    for copy in (kvs_copy, sk_copy):
        copy.wait_send()
    sent(qbuf.at[0, 0, :, pl.ds(0, (NZ - 1) * SHARE), :], zq_send)
    sent(qbuf.at[0, pl.ds(0, NX - 1)], bq_send)
    sent(qbuf.at[pl.ds(0, NX - 1)], aq_send)
    sent(codes.at[pl.ds(0, NX - 1)], rb_send.at[0])
    sent(stats.at[pl.ds(0, NX - 1)], rb_send.at[1])
    sent(ra, ra_send.at[0])
    sent(ras, ra_send.at[1])
    sent(rz, rz_send.at[0])
    sent(rzs, rz_send.at[1])
    half = pl.ds(0, HD // 2)
    sent(anc.at[:, pl.ds(0, (NX - 1) * PROWS), half], bb_send)
    sent(anc.at[:, pl.ds(0, (NX - 1) * AROWS), half], ab_send)
    sent(anc.at[:, :, half], sib_send)

    @pl.when(z == 0)
    def _():
        sent(anc.at[:, pl.ds(0, (NZ - 1) * PROWS // 2), :], zb_send)

        @pl.when(cb == 0)
        def _():
            sent(anc.at[:, pl.ds(0, (NX - 1) * PROWS), half], sb_send)

    @pl.when(is_root)
    def _():
        sent(kv_v.at[:, pl.ds(0, (2 * NX - 1) * AROWS // 2), :], sc_send)

    pltpu.make_async_copy(suf_v, suf_out, suf_sem).wait()
    pltpu.make_async_copy(q_v, ctx_out, out_sem).wait()


def per_device(queries, keys_values, token_ids, lengths, suffix_queries, suffix_kv):
    bf16, f32, i16 = jnp.bfloat16, jnp.float32, jnp.int16
    dma = pltpu.SemaphoreType.DMA
    scratch = [
        pltpu.VMEM((BLK, HD), bf16),
        pltpu.VMEM((2, BLK, HD), bf16),
        pltpu.VMEM((2, BLK, HD), bf16),
        pltpu.VMEM((24, HSZ), jnp.int32),
        pltpu.VMEM((2, HSZ, GH * HSZ), bf16),
        pltpu.VMEM((NX, NX, GH, QB, HSZ), bf16),
        pltpu.VMEM((2, BLK, HD), bf16),
        pltpu.VMEM((NCH, 2, AROWS, CW), bf16),
        pltpu.VMEM((HEADS, BLK, HSZ), f32),
        pltpu.VMEM((HEADS, BLK, HSZ), f32),
        pltpu.VMEM((HEADS, BLK, HSZ), f32),
        pltpu.VMEM((BLK, BLK), f32),
        pltpu.VMEM((1, 2 * BLK), f32),
        pltpu.VMEM((1, BLK), f32),
        pltpu.VMEM((NX, NX, GH, QB, HSZ), i16),
        pltpu.VMEM((NX, NX, 8, HSZ), f32),
        pltpu.VMEM((NX - 1, NX, GH, QB, HSZ), i16),
        pltpu.VMEM((NX - 1, NX, 8, HSZ), f32),
        pltpu.VMEM((NX, GH, QB, HSZ), i16),
        pltpu.VMEM((NX, 8, HSZ), f32),
        pltpu.VMEM((NX - 1, GH, QB, HSZ), i16),
        pltpu.VMEM((NX - 1, 8, HSZ), f32),
        pltpu.VMEM((GH, QB, HSZ), i16),
        pltpu.VMEM((8, HSZ), f32),
        pltpu.VMEM((NZ - 1, GH, SHARE, HSZ), i16),
        pltpu.VMEM((NZ - 1, 8, HSZ), f32),
        pltpu.VMEM((HSZ, HSZ), f32),
        pltpu.VMEM((HEADS, BLK, HSZ), bf16),
        pltpu.VMEM((SHARE, GH * HSZ), bf16),
        dma((5,)),
        dma, dma, dma, dma,
        dma, dma,
        dma, dma,
        dma, dma((NX - 1, NX)),
        dma, dma((NCH,)), dma((NCH,)),
        dma, dma((NCH,)),
        dma, dma((NCH,)),
        dma, dma((NCH,)),
        dma, dma((NCH,)),
        dma, dma((NCH,)),
        dma((2,)), dma((2, NX)),
        dma((2,)), dma((2,)),
        dma((2,)), dma((2,)),
        dma, dma,
    ]
    anywhere = pl.BlockSpec(memory_space=pl.ANY)
    return pl.pallas_call(
        kernel,
        out_shape=(
            pltpu.VMEM((BLK, HD), bf16),
            pltpu.VMEM((SHARE, GH * HSZ), bf16),
        ),
        in_specs=[anywhere, anywhere, anywhere, pl.BlockSpec(memory_space=pltpu.SMEM), anywhere, anywhere],
        out_specs=(anywhere, anywhere),
        scratch_shapes=scratch,
        compiler_params=pltpu.CompilerParams(
            collective_id=0, has_side_effects=True, vmem_limit_bytes=56 * 2**20
        ),
        cost_estimate=pl.CostEstimate(
            flops=6_500_000_000, bytes_accessed=6_500_000, transcendentals=12_600_000
        ),
        name="star",
    )(queries, keys_values, token_ids.reshape(-1, HSZ), lengths, suffix_queries, suffix_kv)


def solution(mesh):
    return jax.shard_map(
        per_device,
        mesh=mesh,
        in_specs=(
            P(("hst", "grp"), None),
            P(None, ("hst", "grp"), None),
            P(),
            P(),
            P("hst", "grp"),
            P(None, "hst", "grp"),
        ),
        out_specs=(P(("hst", "grp"), None), P("hst", "grp")),
        check_vma=False,
    )
```
